512 devices in a mesh: ctx: 16 (over z), kv: 8 (over y, x_lo), qh: 4 (over x_hi, core).
Axes of the slice: x: 4 (x_hi: 2, x_lo: 2; x = x_hi * 2 + x_lo), y: 4, z: 16, core: 2. Of those that a mesh axis runs over, the one named last changes fastest.
Arguments:
- queries: bfloat16 [8, 16, 384, 128], P('kv', 'qh', 'ctx'), may hold values from -16 to 16
- cache_keys: bfloat16 [8, 65536, 128], P('kv', 'ctx'), may hold values from -16 to 16
- cache_values: bfloat16 [8, 65536, 128], P('kv', 'ctx'), may hold values from -6 to 6
- cache_counts: int32 [16], P('ctx'), may hold values from 512 to 4096, as said below
- new_keys: bfloat16 [8, 384, 128], P('kv', ('ctx', 'qh')), may hold values from -16 to 16
- new_values: bfloat16 [8, 384, 128], P('kv', ('ctx', 'qh')), may hold values from -6 to 6
- new_positions: int32 [384], replicated, may hold values from 0 to 383, each once
Outputs:
- attended: bfloat16 [8, 16, 384, 128], P('kv', 'qh', 'ctx')
The draws below stay inside these ranges and needn't reach their ends.
Inputs may be any that keep to these rules, and one draw needn't show every extreme that they name: `cache_counts`: one shard holds 4096 filled slots and another 4096 // 8. `new_positions`: each of 0 to 383 once; all cached tokens precede the new ones.
All inputs are finite; a program needn't handle non-finite values.
Results may differ from the reference program's by a relative error of at most 0.006.
Values may be sent and summed in bfloat16 or wider, within the bound.
A program may use at most 64 MiB of HBM per device.

```python
import jax
import jax.numpy as jnp
from jax import lax

HD = 128
GROUP = 16
KVH = 8
TNEW = 384
CTX_DEV = 4096
CTX = 65536
SHARDS = 16


def draw_queries(key, part):
    key = jax.random.fold_in(key, 11)
    values = jax.random.normal(key, (KVH, GROUP, TNEW, HD), jnp.float32)
    return jnp.clip(values, -16.0, 16.0).astype(jnp.bfloat16)


def draw_cache_keys(key, part):
    key = jax.random.fold_in(key, 12)
    values = jax.random.normal(key, (KVH, CTX, HD), jnp.float32)
    return jnp.clip(values, -16.0, 16.0).astype(jnp.bfloat16)


def draw_new_keys(key, part):
    key = jax.random.fold_in(key, 13)
    values = 2.0 * jax.random.normal(key, (KVH, TNEW, HD), jnp.float32)
    return jnp.clip(values, -16.0, 16.0).astype(jnp.bfloat16)


def draw_cache_counts(key, part):
    key = jax.random.fold_in(key, 14)
    first, second, third = jax.random.split(key, 3)
    filled = jax.random.randint(first, (SHARDS,), CTX_DEV // 8, CTX_DEV + 1).astype(jnp.int32)
    fullest = jax.random.randint(second, (), 0, SHARDS)
    emptiest = (fullest + 1 + jax.random.randint(third, (), 0, SHARDS - 1)) % SHARDS
    filled = filled.at[fullest].set(CTX_DEV)
    filled = filled.at[emptiest].set(CTX_DEV // 8)
    return filled.astype(jnp.int32)


def shard_levels(key, extent, pieces, low, top_value):
    level = 1.0
    for axis_at, parts in pieces:
        heights = jax.random.uniform(jax.random.fold_in(jax.random.fold_in(key, 6), axis_at), (parts,), jnp.float32, low / len(pieces), top_value / len(pieces))
        level = level * jnp.repeat(jnp.exp(heights), extent[axis_at] // parts).reshape((-1,) + (1,) * (len(extent) - 1 - axis_at))
    return level


def gaussian(key, extent, scale, most, shards=(), kind=jnp.bfloat16):
    array = jax.random.normal(key, extent, jnp.float32) * scale
    if len(shards) > 0:
        array = shard_levels(key, extent, shards, -0.22, 0.18) * array
    return jnp.clip(array, min=-most, max=most).astype(kind)


def setup_inputs(seed: int = 0) -> dict:
    key_of = jax.random.split(jax.random.key(seed), 8)
    return {
        "queries": draw_queries(jax.random.fold_in(key_of[7], 71), 0),
        "cache_keys": draw_cache_keys(jax.random.fold_in(key_of[7], 71), 0),
        "cache_values": gaussian(key_of[2], (KVH, CTX, HD), 1.0, 6.0, ((0, 8), (1, 16))),
        "cache_counts": draw_cache_counts(jax.random.fold_in(key_of[7], 71), 0),
        "new_keys": draw_new_keys(jax.random.fold_in(key_of[7], 71), 0),
        "new_values": gaussian(key_of[5], (KVH, TNEW, HD), 1.0, 6.0, ((0, 8), (1, 64))),
        "new_positions": jax.random.permutation(key_of[6], TNEW).astype(jnp.int32),
    }


def attend(query_rows, key_rows, value_rows, allowed):
    scores = lax.dot_general(query_rows, key_rows, (((1,), (1,)), ((), ())), preferred_element_type=jnp.float32) * (key_rows.shape[1] ** -0.5)
    masked = jnp.where(allowed, scores, -jnp.inf)
    highest = jnp.max(masked, axis=1)
    weights = jnp.where(allowed, jnp.exp(scores - highest[:, None]), 0.0).astype(jnp.bfloat16)
    weighted = jnp.dot(weights, value_rows, preferred_element_type=jnp.float32)
    weight_sum = jnp.sum(weights.astype(jnp.float32), axis=1)
    return highest, weighted, weight_sum


def reference(queries, cache_keys, cache_values, cache_counts, new_keys, new_values, new_positions):
    slot_index = jnp.arange(CTX_DEV).astype(jnp.int32)
    row_places = jnp.tile(new_positions, GROUP)
    causal = new_positions[None, :] <= row_places[:, None]

    def one_head(inputs):
        head_queries, head_keys, head_values, fresh_keys, fresh_values = inputs
        query_rows = head_queries.reshape(GROUP * TNEW, HD)
        shard_keys = head_keys.reshape(SHARDS, CTX_DEV, HD)
        shard_values = head_values.reshape(SHARDS, CTX_DEV, HD)

        def per_shard(piece):
            key_rows, value_rows, filled = piece
            return attend(query_rows, key_rows, value_rows, (slot_index < filled)[None, :])

        peaks, sums, masses = lax.map(per_shard, (shard_keys, shard_values, cache_counts))
        fresh_peak, fresh_sum, fresh_mass = attend(query_rows, fresh_keys, fresh_values, causal)
        highest = jnp.maximum(jnp.max(peaks, axis=0), fresh_peak)
        scaling = jnp.exp(peaks - highest[None, :])
        fresh_scale = jnp.exp(fresh_peak - highest)
        numerator = jnp.sum(sums * scaling[:, :, None], axis=0) + fresh_sum * fresh_scale[:, None]
        denominator = jnp.sum(masses * scaling, axis=0) + fresh_mass * fresh_scale
        return (numerator / denominator[:, None]).astype(jnp.bfloat16).reshape(GROUP, TNEW, HD)

    return lax.map(one_head, (queries, cache_keys, cache_values, new_keys, new_values))
```

```python
import functools

import jax
import jax.numpy as jnp
from jax import lax
from jax.experimental import pallas as pl
from jax.experimental.pallas import tpu as pltpu
from jax.sharding import PartitionSpec as P

LOG2E = 1.4426950408889634
TILE = 512
LANES = 128
STATS = 16


def contract(a, b, dims):
    return lax.dot_general(a, b, (dims, ((), ())), preferred_element_type=jnp.float32)


def kernel(
    levels, groups, q_hbm, k_hbm, v_hbm, count_hbm, nk_hbm, nv_hbm, pos_hbm, out_ref,
    q_ref, nk_ref, nv_ref, count_ref, pos_ref, loaded, keys, values, fresh, fresh_keys, fresh_values, wide, place_col, place_row,
    scores, extra, tops, queries, total, peaks,
    hop_out, hop_in, ret_out, ret_in,
    load_sem, fresh_send, fresh_recv, ag_send, ag_recv, hop_send, hop_recv, ret_send, ret_recv,
):
    _, heads, tokens, width = q_ref.shape
    rows = heads * tokens
    slots = keys.shape[1]
    tiles = slots // TILE
    half = levels // 2
    pairs = half // 2
    own_new = nk_ref.shape[1]
    factor = LOG2E * width ** -0.5
    me = lax.axis_index("ctx")
    group = lax.axis_index("qh")

    def level(offset):
        return lax.rem(me + offset + levels, levels)

    def send(src, dst, send_sem, recv_sem, where):
        return pltpu.make_async_remote_copy(
            src_ref=src, dst_ref=dst, send_sem=send_sem, recv_sem=recv_sem,
            device_id=where, device_id_type=pl.DeviceIdType.MESH,
        )

    loads = [
        pltpu.make_async_copy(src, dst, load_sem.at[i])
        for i, (src, dst) in enumerate((
            (q_hbm, q_ref), (nk_hbm, nk_ref), (nv_hbm, nv_ref), (count_hbm, count_ref), (pos_hbm, pos_ref),
            (k_hbm.at[0], loaded), (v_hbm.at[0], values.at[:, 0:width]),
        ))
    ]
    for load in loads:
        load.start()

    barrier = pltpu.get_barrier_semaphore()
    for k in range(pairs):
        for sign in (1, -1):
            pl.semaphore_signal(
                barrier, inc=1, device_id={"ctx": level(sign * (2 * k + 1))}, device_id_type=pl.DeviceIdType.MESH
            )
    for k in range(1, groups):
        pl.semaphore_signal(
            barrier, inc=1, device_id={"qh": lax.rem(group + k, groups)}, device_id_type=pl.DeviceIdType.MESH
        )

    for load in loads[:5]:
        load.wait()
    queries[half - 1, rows:2 * rows, :] = (
        q_ref[0].astype(jnp.float32).reshape(rows, width).astype(jnp.bfloat16)
    )
    wide[...] = jnp.zeros_like(wide)
    wide[0:own_new, :] = nk_ref[0].astype(jnp.float32)
    wide[STATS:STATS + own_new, :] = nv_ref[0].astype(jnp.float32)
    fresh[group] = wide[...].astype(jnp.bfloat16)

    def note_places(j, _):
        for i in range(tokens):
            place_col[pl.ds(j * tokens + i, 1), :] = jnp.full((1, LANES), pos_ref[j * tokens + i], jnp.int32)
        return 0

    lax.fori_loop(0, levels, note_places, 0)
    lane = lax.broadcasted_iota(jnp.int32, (8, LANES), 1)
    row = jnp.full((8, LANES), 1 << 30, jnp.int32)
    for g in range(groups):
        for i in range(own_new):
            place = pos_ref[me * tokens + g * own_new + i]
            row = jnp.where(lane == g * STATS + i, place, row)
    place_row[...] = row

    pl.semaphore_wait(barrier, 2 * pairs + groups - 1)

    own = queries.at[half - 1, rows:2 * rows]

    def right_copy(step, src):
        return send(src, queries.at[step, 0:rows], ag_send.at[0, step], ag_recv.at[0, step], {"ctx": level(1)})

    def left_copy(step, src):
        return send(src, queries.at[step, rows:2 * rows], ag_send.at[1, step], ag_recv.at[1, step], {"ctx": level(-1)})

    right_copy(0, own).start()
    left_copy(0, own).start()

    def fresh_copy(k):
        return send(
            fresh.at[group], fresh.at[group], fresh_send.at[k], fresh_recv.at[group],
            {"qh": lax.rem(group + k, groups)},
        )

    def fresh_arrival(k):
        other = lax.rem(group + k, groups)
        return send(fresh.at[other], fresh.at[other], fresh_send.at[k], fresh_recv.at[other], {"qh": other})

    for k in range(1, groups):
        fresh_copy(k).start()

    count = count_ref[0]
    loads[5].wait()
    loads[6].wait()
    first_key = loaded[0:16, :].astype(jnp.float32)[0:1, :]
    chunk = 256

    def prepare(j, _):
        base = pl.multiple_of(j * chunk, chunk)
        at = pl.ds(base, chunk)
        valid = lax.broadcasted_iota(jnp.int32, (chunk, width), 0) + base < count
        mass = jnp.where(valid, 1.0, 0.0).astype(jnp.bfloat16)
        values[at, width:2 * width] = mass
        values[at, 0:width] = values[at, 0:width] * mass
        chosen = jnp.where(valid, loaded[at, :].astype(jnp.float32), first_key)
        keys[:, at] = chosen.T.astype(jnp.bfloat16)
        return 0

    lax.fori_loop(0, slots // chunk, prepare, 0)

    fresh_keys[...] = jnp.zeros_like(fresh_keys)
    fresh_values[:, 0:width] = jnp.zeros((LANES, width), jnp.bfloat16)
    fresh_values[:, width:2 * width] = jnp.ones((LANES, width), jnp.bfloat16)
    for k in range(1, groups):
        fresh_arrival(k).wait_recv()
    for g in range(groups):
        fresh_keys[g * STATS:(g + 1) * STATS, :] = fresh[g, 0:STATS, :]
        fresh_values[g * STATS:(g + 1) * STATS, 0:width] = fresh[g, STATS:2 * STATS, :]

    def score_tile(step, j):
        at = pl.ds(pl.multiple_of(j * TILE, TILE), TILE)
        made = contract(queries[step], keys[:, at], ((1,), (0,)))
        scores[step % 2, j] = made
        top = tops[...]
        for g in range(TILE // LANES):
            top = jnp.maximum(top, made[:, g * LANES:(g + 1) * LANES])
        tops[...] = top

    def score_start():
        tops[...] = jnp.full(tops.shape, -1e30, jnp.float32)

    def score_end(step):
        made = contract(queries[step], fresh_keys[...], ((1,), (1,)))
        behind = level(-(step + 1))
        ahead = jnp.where(step == half - 1, me, level(step + 1))

        def causal(owner, part):
            place = place_col[pl.ds(pl.multiple_of(owner * tokens, 8), tokens), :]
            place = jnp.concatenate([place] * heads, axis=0)
            limit = jnp.broadcast_to(place_row[0:1, :], place.shape)
            return jnp.where(limit <= place, part, -1e30)

        made = jnp.concatenate([causal(behind, made[0:rows]), causal(ahead, made[rows:])], axis=0)
        extra[step % 2] = made
        top = jnp.max(jnp.maximum(tops[...], made), axis=1, keepdims=True)
        top = top.astype(jnp.bfloat16).astype(jnp.float32)
        peaks[step] = jnp.broadcast_to(top, (2 * rows, LANES))

    def weigh(made, peak):
        return [
            jnp.exp2(made[:, g * LANES:(g + 1) * LANES] * factor - peak)
            for g in range(made.shape[1] // LANES)
        ]

    def weigh_start(step):
        weight = weigh(extra[step % 2], peaks[step] * factor)[0].astype(jnp.bfloat16)
        total[step] = contract(weight, fresh_values[...], ((1,), (0,)))

    def weigh_tile(step, j):
        at = pl.ds(pl.multiple_of(j * TILE, TILE), TILE)
        weight = jnp.concatenate(weigh(scores[step % 2, j], peaks[step] * factor), axis=1).astype(jnp.bfloat16)
        total[step] += contract(weight, values[at, :], ((1,), (0,)))

    eye = lax.broadcasted_iota(jnp.int32, (rows, LANES), 0) == lax.broadcasted_iota(jnp.int32, (rows, LANES), 1)

    def pack(ref, part):
        number, mass, peak = part
        ref[0:rows, :] = number.astype(jnp.bfloat16)
        peak_row = jnp.sum(jnp.where(eye, peak, 0.0), axis=0, keepdims=True)
        mass_row = jnp.sum(jnp.where(eye, mass, 0.0), axis=0, keepdims=True)
        mass_high = mass_row.astype(jnp.bfloat16).astype(jnp.float32)
        line = lax.broadcasted_iota(jnp.int32, (STATS, LANES), 0)
        stats = jnp.where(
            line == 0, peak_row, jnp.where(line == 1, mass_high, jnp.where(line == 2, mass_row - mass_high, 0.0))
        )
        ref[rows:rows + STATS, :] = stats.astype(jnp.bfloat16)

    def unpack(ref):
        number = ref[0:rows, :].astype(jnp.float32)
        stats = ref[rows:rows + STATS, :].astype(jnp.float32)

        def column(line):
            spread = jnp.where(eye, jnp.broadcast_to(line, (rows, LANES)), 0.0)
            return jnp.broadcast_to(jnp.sum(spread, axis=1, keepdims=True), (rows, LANES))

        return number, column(stats[1:2, :] + stats[2:3, :]), column(stats[0:1, :])

    def local(step, side):
        at = slice(side * rows, (side + 1) * rows)
        return total[step, at, 0:width], total[step, at, width:2 * width], peaks[step, at, :]

    def merge(a, b):
        peak = jnp.maximum(a[2], b[2])
        wa = jnp.exp2((a[2] - peak) * factor)
        wb = jnp.exp2((b[2] - peak) * factor)
        return a[0] * wa + b[0] * wb, a[1] * wa + b[1] * wb, peak

    def hop_copy(side, k):
        return send(
            hop_out.at[side, k], hop_in.at[side, k], hop_send.at[side, k], hop_recv.at[side, k],
            {"ctx": level(-1 if side == 0 else 1)},
        )

    def ret_copy(side, k):
        distance = 2 * k + 1
        return send(
            ret_out.at[side, k], ret_in.at[side, k], ret_send.at[side, k], ret_recv.at[side, k],
            {"ctx": level(-distance if side == 0 else distance)},
        )

    def pass_on(side, k):
        pack(hop_out.at[side, k], local(2 * k + 1, side))
        hop_copy(side, k).start()

    def return_pair(side, k):
        hop_copy(side, k).wait_recv()
        pack(ret_out.at[side, k], merge(local(2 * k, side), unpack(hop_in.at[side, k])))
        ret_copy(side, k).start()

    def forward(step):
        right_copy(step, queries.at[step, 0:rows]).wait_recv()

        @pl.when(step < half - 1)
        def _():
            right_copy(step + 1, queries.at[step, 0:rows]).start()
            left_copy(step, queries.at[step, rows:2 * rows]).wait_recv()

        @pl.when(step < half - 2)
        def _():
            left_copy(step + 1, queries.at[step, rows:2 * rows]).start()

    forward(0)
    score_start()

    def first(j, _):
        score_tile(0, j)
        return 0

    lax.fori_loop(0, tiles, first, 0)
    score_end(0)

    def turn(step, _):
        forward(step + 1)
        score_start()
        weigh_start(step)

        def both(j, _):
            score_tile(step + 1, j)
            weigh_tile(step, j)
            return 0

        lax.fori_loop(0, tiles, both, 0)
        score_end(step + 1)

        @pl.when(step % 2 == 1)
        def _():
            pass_on(0, step // 2)
            pass_on(1, step // 2)

        @pl.when((step % 2 == 0) & (step >= 2))
        def _():
            return_pair(0, step // 2 - 1)
            return_pair(1, step // 2 - 1)

        return 0

    lax.fori_loop(0, half - 1, turn, 0)
    pack(ret_out.at[1, pairs - 1], local(half - 2, 1))
    ret_copy(1, pairs - 1).start()
    weigh_start(half - 1)

    def last(j, _):
        weigh_tile(half - 1, j)
        return 0

    lax.fori_loop(0, tiles, last, 0)
    pass_on(0, pairs - 1)
    result = local(half - 1, 1)
    for k in range(pairs - 1):
        for side in (0, 1):
            ret_copy(side, k).wait_recv()
            result = merge(result, unpack(ret_in.at[side, k]))
    return_pair(0, pairs - 1)
    for side in (1, 0):
        ret_copy(side, pairs - 1).wait_recv()
        result = merge(result, unpack(ret_in.at[side, pairs - 1]))
    out_ref[0] = (result[0] / result[1]).reshape(heads, tokens, width).astype(jnp.bfloat16)

    for step in range(half):
        right_copy(step, own).wait_send()
        if step < half - 1:
            left_copy(step, own).wait_send()
    for k in range(1, groups):
        fresh_copy(k).wait_send()
    for k in range(pairs):
        for side in (0, 1):
            ret_copy(side, k).wait_send()
            if (side, k) != (1, pairs - 1):
                hop_copy(side, k).wait_send()


def per_device(queries, cache_keys, cache_values, cache_counts, new_keys, new_values, new_positions):
    levels = lax.axis_size("ctx")
    groups = lax.axis_size("qh")
    _, heads, tokens, width = queries.shape
    slots = cache_keys.shape[1]
    rows = heads * tokens
    half = levels // 2
    pairs = half // 2
    vmem = pl.BlockSpec(memory_space=pltpu.VMEM)
    anywhere = pl.BlockSpec(memory_space=pl.ANY)
    packed = rows + STATS
    dma = pltpu.SemaphoreType.DMA
    scratch = [
        pltpu.VMEM(queries.shape, queries.dtype),
        pltpu.VMEM(new_keys.shape, new_keys.dtype),
        pltpu.VMEM(new_values.shape, new_values.dtype),
        pltpu.SMEM(cache_counts.shape, cache_counts.dtype),
        pltpu.SMEM(new_positions.shape, new_positions.dtype),
        pltpu.VMEM((slots, width), jnp.bfloat16),
        pltpu.VMEM((width, slots), jnp.bfloat16),
        pltpu.VMEM((slots, 2 * width), jnp.bfloat16),
        pltpu.VMEM((groups, 2 * STATS, width), jnp.bfloat16),
        pltpu.VMEM((LANES, width), jnp.bfloat16),
        pltpu.VMEM((LANES, 2 * width), jnp.bfloat16),
        pltpu.VMEM((2 * STATS, width), jnp.float32),
        pltpu.VMEM((levels * tokens, LANES), jnp.int32),
        pltpu.VMEM((8, LANES), jnp.int32),
        pltpu.VMEM((2, slots // TILE, 2 * rows, TILE), jnp.float32),
        pltpu.VMEM((2, 2 * rows, LANES), jnp.float32),
        pltpu.VMEM((2 * rows, LANES), jnp.float32),
        pltpu.VMEM((half, 2 * rows, width), jnp.bfloat16),
        pltpu.VMEM((half, 2 * rows, 2 * width), jnp.float32),
        pltpu.VMEM((half, 2 * rows, LANES), jnp.float32),
        pltpu.VMEM((2, pairs, packed, width), jnp.bfloat16),
        pltpu.VMEM((2, pairs, packed, width), jnp.bfloat16),
        pltpu.VMEM((2, pairs, packed, width), jnp.bfloat16),
        pltpu.VMEM((2, pairs, packed, width), jnp.bfloat16),
        dma((7,)),
        dma((groups,)),
        dma((groups,)),
        dma((2, half)),
        dma((2, half)),
        dma((2, pairs)),
        dma((2, pairs)),
        dma((2, pairs)),
        dma((2, pairs)),
    ]
    return pl.pallas_call(
        functools.partial(kernel, levels, groups),
        out_shape=jax.ShapeDtypeStruct(queries.shape, queries.dtype),
        in_specs=[anywhere] * 7,
        out_specs=vmem,
        scratch_shapes=scratch,
        compiler_params=pltpu.CompilerParams(
            collective_id=0, has_side_effects=True, vmem_limit_bytes=60 * 1024 * 1024
        ),
        cost_estimate=pl.CostEstimate(
            flops=4 * levels * rows * slots * width,
            bytes_accessed=4 * slots * width,
            transcendentals=levels * rows * slots,
        ),
        name="ring_attention",
    )(queries, cache_keys, cache_values, cache_counts, new_keys, new_values, new_positions)


def solution(mesh):
    placed = (
        P("kv", "qh", "ctx", None),
        P("kv", "ctx", None),
        P("kv", "ctx", None),
        P("ctx"),
        P("kv", ("ctx", "qh"), None),
        P("kv", ("ctx", "qh"), None),
        P(),
    )
    return jax.shard_map(
        per_device,
        mesh=mesh,
        in_specs=placed,
        out_specs=P("kv", "qh", "ctx", None),
        check_vma=False,
    )
```

```python
import functools

import jax
import jax.numpy as jnp
from jax import lax
from jax.experimental import pallas as pl
from jax.experimental.pallas import tpu as pltpu
from jax.sharding import PartitionSpec as P

LOG2E = 1.4426950408889634
TILE = 2048
LANES = 128
STATS = 16


def contract(a, b, dims):
    return lax.dot_general(a, b, (dims, ((), ())), preferred_element_type=jnp.float32)


def kernel(
    levels, groups, q_hbm, k_hbm, v_hbm, count_hbm, nk_hbm, nv_hbm, pos_hbm, out_ref,
    q_ref, nk_ref, nv_ref, count_ref, pos_ref, loaded, keys, values, fresh, fresh_keys, fresh_values, wide, place_col, place_row,
    scores, extra, tops, queries, total, peaks,
    hop_out, hop_in, ret_out, ret_in,
    load_sem, fresh_send, fresh_recv, ag_send, ag_recv, hop_send, hop_recv, ret_send, ret_recv,
):
    _, heads, tokens, width = q_ref.shape
    rows = heads * tokens
    slots = keys.shape[1]
    tiles = slots // TILE
    half = levels // 2
    pairs = half // 2
    own_new = nk_ref.shape[1]
    factor = LOG2E * width ** -0.5
    me = lax.axis_index("ctx")
    group = lax.axis_index("qh")

    def level(offset):
        return lax.rem(me + offset + levels, levels)

    def send(src, dst, send_sem, recv_sem, where):
        return pltpu.make_async_remote_copy(
            src_ref=src, dst_ref=dst, send_sem=send_sem, recv_sem=recv_sem,
            device_id=where, device_id_type=pl.DeviceIdType.MESH,
        )

    loads = [
        pltpu.make_async_copy(src, dst, load_sem.at[i])
        for i, (src, dst) in enumerate((
            (q_hbm, q_ref), (nk_hbm, nk_ref), (nv_hbm, nv_ref), (count_hbm, count_ref), (pos_hbm, pos_ref),
            (k_hbm.at[0], loaded), (v_hbm.at[0], values.at[:, 0:width]),
        ))
    ]
    for load in loads:
        load.start()

    barrier = pltpu.get_barrier_semaphore()
    for k in range(pairs):
        for sign in (1, -1):
            pl.semaphore_signal(
                barrier, inc=1, device_id={"ctx": level(sign * (2 * k + 1))}, device_id_type=pl.DeviceIdType.MESH
            )
    for k in range(1, groups):
        pl.semaphore_signal(
            barrier, inc=1, device_id={"qh": lax.rem(group + k, groups)}, device_id_type=pl.DeviceIdType.MESH
        )

    for load in loads[:5]:
        load.wait()
    queries[half - 1, rows:2 * rows, :] = (
        q_ref[0].astype(jnp.float32).reshape(rows, width).astype(jnp.bfloat16)
    )
    wide[...] = jnp.zeros_like(wide)
    wide[0:own_new, :] = nk_ref[0].astype(jnp.float32)
    wide[STATS:STATS + own_new, :] = nv_ref[0].astype(jnp.float32)
    fresh[group] = wide[...].astype(jnp.bfloat16)

    def note_places(j, _):
        for i in range(tokens):
            place_col[pl.ds(j * tokens + i, 1), :] = jnp.full((1, LANES), pos_ref[j * tokens + i], jnp.int32)
        return 0

    lax.fori_loop(0, levels, note_places, 0)
    lane = lax.broadcasted_iota(jnp.int32, (8, LANES), 1)
    row = jnp.full((8, LANES), 1 << 30, jnp.int32)
    for g in range(groups):
        for i in range(own_new):
            place = pos_ref[me * tokens + g * own_new + i]
            row = jnp.where(lane == g * STATS + i, place, row)
    place_row[...] = row

    pl.semaphore_wait(barrier, 2 * pairs + groups - 1)

    own = queries.at[half - 1, rows:2 * rows]

    def right_copy(step, src):
        return send(src, queries.at[step, 0:rows], ag_send.at[0, step], ag_recv.at[0, step], {"ctx": level(1)})

    def left_copy(step, src):
        return send(src, queries.at[step, rows:2 * rows], ag_send.at[1, step], ag_recv.at[1, step], {"ctx": level(-1)})

    right_copy(0, own).start()
    left_copy(0, own).start()

    def fresh_copy(k):
        return send(
            fresh.at[group], fresh.at[group], fresh_send.at[k], fresh_recv.at[group],
            {"qh": lax.rem(group + k, groups)},
        )

    def fresh_arrival(k):
        other = lax.rem(group + k, groups)
        return send(fresh.at[other], fresh.at[other], fresh_send.at[k], fresh_recv.at[other], {"qh": other})

    for k in range(1, groups):
        fresh_copy(k).start()

    count = count_ref[0]
    loads[5].wait()
    loads[6].wait()
    first_key = loaded[0:16, :].astype(jnp.float32)[0:1, :]
    chunk = 256

    def prepare(j, _):
        base = pl.multiple_of(j * chunk, chunk)
        at = pl.ds(base, chunk)
        valid = lax.broadcasted_iota(jnp.int32, (chunk, width), 0) + base < count
        mass = jnp.where(valid, 1.0, 0.0).astype(jnp.bfloat16)
        values[at, width:2 * width] = mass
        values[at, 0:width] = values[at, 0:width] * mass
        chosen = jnp.where(valid, loaded[at, :].astype(jnp.float32), first_key)
        keys[:, at] = chosen.T.astype(jnp.bfloat16)
        return 0

    lax.fori_loop(0, slots // chunk, prepare, 0)

    fresh_keys[...] = jnp.zeros_like(fresh_keys)
    fresh_values[:, 0:width] = jnp.zeros((LANES, width), jnp.bfloat16)
    fresh_values[:, width:2 * width] = jnp.ones((LANES, width), jnp.bfloat16)
    for k in range(1, groups):
        fresh_arrival(k).wait_recv()
    for g in range(groups):
        fresh_keys[g * STATS:(g + 1) * STATS, :] = fresh[g, 0:STATS, :]
        fresh_values[g * STATS:(g + 1) * STATS, 0:width] = fresh[g, STATS:2 * STATS, :]

    def score_tile(step, j):
        at = pl.ds(pl.multiple_of(j * TILE, TILE), TILE)
        made = contract(queries[step], keys[:, at], ((1,), (0,)))
        scores[step % 2, j] = made
        top = tops[...]
        for g in range(TILE // LANES):
            top = jnp.maximum(top, made[:, g * LANES:(g + 1) * LANES])
        tops[...] = top

    def score_start():
        tops[...] = jnp.full(tops.shape, -1e30, jnp.float32)

    def score_end(step):
        made = contract(queries[step], fresh_keys[...], ((1,), (1,)))
        behind = level(-(step + 1))
        ahead = jnp.where(step == half - 1, me, level(step + 1))

        def causal(owner, part):
            place = place_col[pl.ds(pl.multiple_of(owner * tokens, 8), tokens), :]
            place = jnp.concatenate([place] * heads, axis=0)
            limit = jnp.broadcast_to(place_row[0:1, :], place.shape)
            return jnp.where(limit <= place, part, -1e30)

        made = jnp.concatenate([causal(behind, made[0:rows]), causal(ahead, made[rows:])], axis=0)
        extra[step % 2] = made
        top = jnp.max(jnp.maximum(tops[...], made), axis=1, keepdims=True)
        top = top.astype(jnp.bfloat16).astype(jnp.float32)
        peaks[step] = jnp.broadcast_to(top, (2 * rows, LANES))

    def weigh(made, peak):
        return [
            jnp.exp2(made[:, g * LANES:(g + 1) * LANES] * factor - peak)
            for g in range(made.shape[1] // LANES)
        ]

    def weigh_start(step):
        weight = weigh(extra[step % 2], peaks[step] * factor)[0].astype(jnp.bfloat16)
        total[step] = contract(weight, fresh_values[...], ((1,), (0,)))

    def weigh_tile(step, j):
        at = pl.ds(pl.multiple_of(j * TILE, TILE), TILE)
        weight = jnp.concatenate(weigh(scores[step % 2, j], peaks[step] * factor), axis=1).astype(jnp.bfloat16)
        total[step] += contract(weight, values[at, :], ((1,), (0,)))

    eye = lax.broadcasted_iota(jnp.int32, (rows, LANES), 0) == lax.broadcasted_iota(jnp.int32, (rows, LANES), 1)

    def pack(ref, part):
        number, mass, peak = part
        ref[0:rows, :] = number.astype(jnp.bfloat16)
        peak_row = jnp.sum(jnp.where(eye, peak, 0.0), axis=0, keepdims=True)
        mass_row = jnp.sum(jnp.where(eye, mass, 0.0), axis=0, keepdims=True)
        mass_high = mass_row.astype(jnp.bfloat16).astype(jnp.float32)
        line = lax.broadcasted_iota(jnp.int32, (STATS, LANES), 0)
        stats = jnp.where(
            line == 0, peak_row, jnp.where(line == 1, mass_high, jnp.where(line == 2, mass_row - mass_high, 0.0))
        )
        ref[rows:rows + STATS, :] = stats.astype(jnp.bfloat16)

    def unpack(ref):
        number = ref[0:rows, :].astype(jnp.float32)
        stats = ref[rows:rows + STATS, :].astype(jnp.float32)

        def column(line):
            spread = jnp.where(eye, jnp.broadcast_to(line, (rows, LANES)), 0.0)
            return jnp.broadcast_to(jnp.sum(spread, axis=1, keepdims=True), (rows, LANES))

        return number, column(stats[1:2, :] + stats[2:3, :]), column(stats[0:1, :])

    def local(step, side):
        at = slice(side * rows, (side + 1) * rows)
        return total[step, at, 0:width], total[step, at, width:2 * width], peaks[step, at, :]

    def merge(a, b):
        peak = jnp.maximum(a[2], b[2])
        wa = jnp.exp2((a[2] - peak) * factor)
        wb = jnp.exp2((b[2] - peak) * factor)
        return a[0] * wa + b[0] * wb, a[1] * wa + b[1] * wb, peak

    def hop_copy(side, k):
        return send(
            hop_out.at[side, k], hop_in.at[side, k], hop_send.at[side, k], hop_recv.at[side, k],
            {"ctx": level(-1 if side == 0 else 1)},
        )

    def ret_copy(side, k):
        distance = 2 * k + 1
        return send(
            ret_out.at[side, k], ret_in.at[side, k], ret_send.at[side, k], ret_recv.at[side, k],
            {"ctx": level(-distance if side == 0 else distance)},
        )

    def pass_on(side, k):
        pack(hop_out.at[side, k], local(2 * k + 1, side))
        hop_copy(side, k).start()

    def return_pair(side, k):
        hop_copy(side, k).wait_recv()
        pack(ret_out.at[side, k], merge(local(2 * k, side), unpack(hop_in.at[side, k])))
        ret_copy(side, k).start()

    def forward(step):
        right_copy(step, queries.at[step, 0:rows]).wait_recv()

        @pl.when(step < half - 1)
        def _():
            right_copy(step + 1, queries.at[step, 0:rows]).start()
            left_copy(step, queries.at[step, rows:2 * rows]).wait_recv()

        @pl.when(step < half - 2)
        def _():
            left_copy(step + 1, queries.at[step, rows:2 * rows]).start()

    forward(0)
    score_start()

    def first(j, _):
        score_tile(0, j)
        return 0

    lax.fori_loop(0, tiles, first, 0)
    score_end(0)

    def turn(step, _):
        forward(step + 1)
        score_start()
        weigh_start(step)

        def both(j, _):
            score_tile(step + 1, j)
            weigh_tile(step, j)
            return 0

        lax.fori_loop(0, tiles, both, 0)
        score_end(step + 1)

        @pl.when(step % 2 == 1)
        def _():
            pass_on(0, step // 2)
            pass_on(1, step // 2)

        @pl.when((step % 2 == 0) & (step >= 2))
        def _():
            return_pair(0, step // 2 - 1)
            return_pair(1, step // 2 - 1)

        return 0

    lax.fori_loop(0, half - 1, turn, 0)
    pack(ret_out.at[1, pairs - 1], local(half - 2, 1))
    ret_copy(1, pairs - 1).start()
    weigh_start(half - 1)

    def last(j, _):
        weigh_tile(half - 1, j)
        return 0

    lax.fori_loop(0, tiles, last, 0)
    pass_on(0, pairs - 1)
    result = local(half - 1, 1)
    for k in range(pairs - 1):
        for side in (0, 1):
            ret_copy(side, k).wait_recv()
            result = merge(result, unpack(ret_in.at[side, k]))
    return_pair(0, pairs - 1)
    for side in (1, 0):
        ret_copy(side, pairs - 1).wait_recv()
        result = merge(result, unpack(ret_in.at[side, pairs - 1]))
    out_ref[0] = (result[0] / result[1]).reshape(heads, tokens, width).astype(jnp.bfloat16)

    for step in range(half):
        right_copy(step, own).wait_send()
        if step < half - 1:
            left_copy(step, own).wait_send()
    for k in range(1, groups):
        fresh_copy(k).wait_send()
    for k in range(pairs):
        for side in (0, 1):
            ret_copy(side, k).wait_send()
            if (side, k) != (1, pairs - 1):
                hop_copy(side, k).wait_send()


def per_device(queries, cache_keys, cache_values, cache_counts, new_keys, new_values, new_positions):
    levels = lax.axis_size("ctx")
    groups = lax.axis_size("qh")
    _, heads, tokens, width = queries.shape
    slots = cache_keys.shape[1]
    rows = heads * tokens
    half = levels // 2
    pairs = half // 2
    vmem = pl.BlockSpec(memory_space=pltpu.VMEM)
    anywhere = pl.BlockSpec(memory_space=pl.ANY)
    packed = rows + STATS
    dma = pltpu.SemaphoreType.DMA
    scratch = [
        pltpu.VMEM(queries.shape, queries.dtype),
        pltpu.VMEM(new_keys.shape, new_keys.dtype),
        pltpu.VMEM(new_values.shape, new_values.dtype),
        pltpu.SMEM(cache_counts.shape, cache_counts.dtype),
        pltpu.SMEM(new_positions.shape, new_positions.dtype),
        pltpu.VMEM((slots, width), jnp.bfloat16),
        pltpu.VMEM((width, slots), jnp.bfloat16),
        pltpu.VMEM((slots, 2 * width), jnp.bfloat16),
        pltpu.VMEM((groups, 2 * STATS, width), jnp.bfloat16),
        pltpu.VMEM((LANES, width), jnp.bfloat16),
        pltpu.VMEM((LANES, 2 * width), jnp.bfloat16),
        pltpu.VMEM((2 * STATS, width), jnp.float32),
        pltpu.VMEM((levels * tokens, LANES), jnp.int32),
        pltpu.VMEM((8, LANES), jnp.int32),
        pltpu.VMEM((2, slots // TILE, 2 * rows, TILE), jnp.float32),
        pltpu.VMEM((2, 2 * rows, LANES), jnp.float32),
        pltpu.VMEM((2 * rows, LANES), jnp.float32),
        pltpu.VMEM((half, 2 * rows, width), jnp.bfloat16),
        pltpu.VMEM((half, 2 * rows, 2 * width), jnp.float32),
        pltpu.VMEM((half, 2 * rows, LANES), jnp.float32),
        pltpu.VMEM((2, pairs, packed, width), jnp.bfloat16),
        pltpu.VMEM((2, pairs, packed, width), jnp.bfloat16),
        pltpu.VMEM((2, pairs, packed, width), jnp.bfloat16),
        pltpu.VMEM((2, pairs, packed, width), jnp.bfloat16),
        dma((7,)),
        dma((groups,)),
        dma((groups,)),
        dma((2, half)),
        dma((2, half)),
        dma((2, pairs)),
        dma((2, pairs)),
        dma((2, pairs)),
        dma((2, pairs)),
    ]
    return pl.pallas_call(
        functools.partial(kernel, levels, groups),
        out_shape=jax.ShapeDtypeStruct(queries.shape, queries.dtype),
        in_specs=[anywhere] * 7,
        out_specs=vmem,
        scratch_shapes=scratch,
        compiler_params=pltpu.CompilerParams(
            collective_id=0, has_side_effects=True, vmem_limit_bytes=60 * 1024 * 1024
        ),
        cost_estimate=pl.CostEstimate(
            flops=4 * levels * rows * slots * width,
            bytes_accessed=4 * slots * width,
            transcendentals=levels * rows * slots,
        ),
        name="ring_attention",
    )(queries, cache_keys, cache_values, cache_counts, new_keys, new_values, new_positions)


def solution(mesh):
    placed = (
        P("kv", "qh", "ctx", None),
        P("kv", "ctx", None),
        P("kv", "ctx", None),
        P("ctx"),
        P("kv", ("ctx", "qh"), None),
        P("kv", ("ctx", "qh"), None),
        P(),
    )
    return jax.shard_map(
        per_device,
        mesh=mesh,
        in_specs=placed,
        out_specs=P("kv", "qh", "ctx", None),
        check_vma=False,
    )
```

```python
import functools

import jax
import jax.numpy as jnp
from jax import lax
from jax.experimental import pallas as pl
from jax.experimental.pallas import tpu as pltpu
from jax.sharding import PartitionSpec as P

LOG2E = 1.4426950408889634
TILE = 2048
LANES = 128
STATS = 16


def contract(a, b, dims):
    return lax.dot_general(a, b, (dims, ((), ())), preferred_element_type=jnp.float32)


def kernel(
    levels, groups, q_hbm, k_hbm, v_hbm, count_hbm, nk_hbm, nv_hbm, pos_hbm, out_ref,
    q_ref, nk_ref, nv_ref, count_ref, pos_ref, loaded, keys, values, fresh, fresh_keys, fresh_values, wide, place_col, place_row,
    scores, extra, tops, queries, total, peaks,
    sent, landed,
    load_sem, fresh_send, fresh_recv, ag_send, ag_recv, back_send, back_recv,
):
    _, heads, tokens, width = q_ref.shape
    rows = heads * tokens
    slots = keys.shape[1]
    tiles = slots // TILE
    half = levels // 2
    near = half // 2
    own_new = nk_ref.shape[1]
    factor = LOG2E * width ** -0.5
    me = lax.axis_index("ctx")
    group = lax.axis_index("qh")

    def level(offset):
        return lax.rem(me + offset + levels, levels)

    def send(src, dst, send_sem, recv_sem, where):
        return pltpu.make_async_remote_copy(
            src_ref=src, dst_ref=dst, send_sem=send_sem, recv_sem=recv_sem,
            device_id=where, device_id_type=pl.DeviceIdType.MESH,
        )

    loads = [
        pltpu.make_async_copy(src, dst, load_sem.at[i])
        for i, (src, dst) in enumerate((
            (q_hbm, q_ref), (nk_hbm, nk_ref), (nv_hbm, nv_ref), (count_hbm, count_ref), (pos_hbm, pos_ref),
            (k_hbm.at[0], loaded), (v_hbm.at[0], values.at[:, 0:width]),
        ))
    ]
    for load in loads:
        load.start()

    barrier = pltpu.get_barrier_semaphore()
    for distance in (1, -1, near + 1, -near - 1):
        pl.semaphore_signal(barrier, inc=1, device_id={"ctx": level(distance)}, device_id_type=pl.DeviceIdType.MESH)
    for k in range(1, groups):
        pl.semaphore_signal(
            barrier, inc=1, device_id={"qh": lax.rem(group + k, groups)}, device_id_type=pl.DeviceIdType.MESH
        )

    for load in loads[:5]:
        load.wait()
    queries[half - 1, rows:2 * rows, :] = (
        q_ref[0].astype(jnp.float32).reshape(rows, width).astype(jnp.bfloat16)
    )
    wide[...] = jnp.zeros_like(wide)
    wide[0:own_new, :] = nk_ref[0].astype(jnp.float32)
    wide[STATS:STATS + own_new, :] = nv_ref[0].astype(jnp.float32)
    fresh[group] = wide[...].astype(jnp.bfloat16)

    def note_places(j, _):
        for i in range(tokens):
            place_col[pl.ds(j * tokens + i, 1), :] = jnp.full((1, LANES), pos_ref[j * tokens + i], jnp.int32)
        return 0

    lax.fori_loop(0, levels, note_places, 0)
    lane = lax.broadcasted_iota(jnp.int32, (8, LANES), 1)
    row = jnp.full((8, LANES), 1 << 30, jnp.int32)
    for g in range(groups):
        for i in range(own_new):
            place = pos_ref[me * tokens + g * own_new + i]
            row = jnp.where(lane == g * STATS + i, place, row)
    place_row[...] = row

    pl.semaphore_wait(barrier, 4 + groups - 1)

    own = queries.at[half - 1, rows:2 * rows]

    def right_copy(step, src):
        return send(src, queries.at[step, 0:rows], ag_send.at[0, step], ag_recv.at[0, step], {"ctx": level(1)})

    def left_copy(step, src):
        return send(src, queries.at[step, rows:2 * rows], ag_send.at[1, step], ag_recv.at[1, step], {"ctx": level(-1)})

    right_copy(0, own).start()
    left_copy(0, own).start()

    def fresh_copy(k):
        return send(
            fresh.at[group], fresh.at[group], fresh_send.at[k], fresh_recv.at[group],
            {"qh": lax.rem(group + k, groups)},
        )

    def fresh_arrival(k):
        other = lax.rem(group + k, groups)
        return send(fresh.at[other], fresh.at[other], fresh_send.at[k], fresh_recv.at[other], {"qh": other})

    for k in range(1, groups):
        fresh_copy(k).start()

    count = count_ref[0]
    loads[5].wait()
    loads[6].wait()
    first_key = loaded[0:16, :].astype(jnp.float32)[0:1, :]
    chunk = 256

    def prepare(j, _):
        base = pl.multiple_of(j * chunk, chunk)
        at = pl.ds(base, chunk)
        valid = lax.broadcasted_iota(jnp.int32, (chunk, width), 0) + base < count
        mass = jnp.where(valid, 1.0, 0.0).astype(jnp.bfloat16)
        values[at, width:2 * width] = mass
        values[at, 0:width] = values[at, 0:width] * mass
        chosen = jnp.where(valid, loaded[at, :].astype(jnp.float32), first_key)
        keys[:, at] = chosen.T.astype(jnp.bfloat16)
        return 0

    lax.fori_loop(0, slots // chunk, prepare, 0)

    fresh_keys[...] = jnp.zeros_like(fresh_keys)
    fresh_values[:, 0:width] = jnp.zeros((LANES, width), jnp.bfloat16)
    fresh_values[:, width:2 * width] = jnp.ones((LANES, width), jnp.bfloat16)
    for k in range(1, groups):
        fresh_arrival(k).wait_recv()
    for g in range(groups):
        fresh_keys[g * STATS:(g + 1) * STATS, :] = fresh[g, 0:STATS, :]
        fresh_values[g * STATS:(g + 1) * STATS, 0:width] = fresh[g, STATS:2 * STATS, :]

    def score_tile(step, j):
        at = pl.ds(pl.multiple_of(j * TILE, TILE), TILE)
        made = contract(queries[step], keys[:, at], ((1,), (0,)))
        scores[step % 2, j] = made
        top = tops[...]
        for g in range(TILE // LANES):
            top = jnp.maximum(top, made[:, g * LANES:(g + 1) * LANES])
        tops[...] = top

    def score_start():
        tops[...] = jnp.full(tops.shape, -1e30, jnp.float32)

    def score_end(step):
        made = contract(queries[step], fresh_keys[...], ((1,), (1,)))
        behind = level(-(step + 1))
        ahead = jnp.where(step == half - 1, me, level(step + 1))

        def causal(owner, part):
            place = place_col[pl.ds(pl.multiple_of(owner * tokens, 8), tokens), :]
            place = jnp.concatenate([place] * heads, axis=0)
            limit = jnp.broadcast_to(place_row[0:1, :], place.shape)
            return jnp.where(limit <= place, part, -1e30)

        made = jnp.concatenate([causal(behind, made[0:rows]), causal(ahead, made[rows:])], axis=0)
        extra[step % 2] = made
        top = jnp.max(jnp.maximum(tops[...], made), axis=1, keepdims=True)
        top = top.astype(jnp.bfloat16).astype(jnp.float32)
        peaks[step] = jnp.broadcast_to(top, (2 * rows, LANES))

    def weigh(made, peak):
        return [
            jnp.exp2(made[:, g * LANES:(g + 1) * LANES] * factor - peak)
            for g in range(made.shape[1] // LANES)
        ]

    def weigh_start(step):
        weight = weigh(extra[step % 2], peaks[step] * factor)[0].astype(jnp.bfloat16)
        total[step] = contract(weight, fresh_values[...], ((1,), (0,)))

    def weigh_tile(step, j):
        at = pl.ds(pl.multiple_of(j * TILE, TILE), TILE)
        weight = jnp.concatenate(weigh(scores[step % 2, j], peaks[step] * factor), axis=1).astype(jnp.bfloat16)
        total[step] += contract(weight, values[at, :], ((1,), (0,)))

    eye = lax.broadcasted_iota(jnp.int32, (rows, LANES), 0) == lax.broadcasted_iota(jnp.int32, (rows, LANES), 1)

    def pack(ref, part):
        number, mass, peak = part
        ref[0:rows, :] = number.astype(jnp.bfloat16)
        peak_row = jnp.sum(jnp.where(eye, peak, 0.0), axis=0, keepdims=True)
        mass_row = jnp.sum(jnp.where(eye, mass, 0.0), axis=0, keepdims=True)
        mass_high = mass_row.astype(jnp.bfloat16).astype(jnp.float32)
        line = lax.broadcasted_iota(jnp.int32, (STATS, LANES), 0)
        stats = jnp.where(
            line == 0, peak_row, jnp.where(line == 1, mass_high, jnp.where(line == 2, mass_row - mass_high, 0.0))
        )
        ref[rows:rows + STATS, :] = stats.astype(jnp.bfloat16)

    def unpack(ref):
        number = ref[0:rows, :].astype(jnp.float32)
        stats = ref[rows:rows + STATS, :].astype(jnp.float32)

        def column(line):
            spread = jnp.where(eye, jnp.broadcast_to(line, (rows, LANES)), 0.0)
            return jnp.broadcast_to(jnp.sum(spread, axis=1, keepdims=True), (rows, LANES))

        return number, column(stats[1:2, :] + stats[2:3, :]), column(stats[0:1, :])

    def local(step, side):
        at = slice(side * rows, (side + 1) * rows)
        return total[step, at, 0:width], total[step, at, width:2 * width], peaks[step, at, :]

    def merge(a, b):
        peak = jnp.maximum(a[2], b[2])
        wa = jnp.exp2((a[2] - peak) * factor)
        wb = jnp.exp2((b[2] - peak) * factor)
        return a[0] * wa + b[0] * wb, a[1] * wa + b[1] * wb, peak

    def back_copy(side, step):
        hop = jnp.where(step == near, near + 1, 1)
        return send(
            sent.at[side, step], landed.at[side, step], back_send.at[side, step], back_recv.at[side, step],
            {"ctx": level(-hop if side == 0 else hop)},
        )

    def pass_first(side, step):
        pack(sent.at[side, step], local(step, side))
        back_copy(side, step).start()

    def pass_merged(side, step):
        back_copy(side, step + 1).wait_recv()
        pack(sent.at[side, step], merge(local(step, side), unpack(landed.at[side, step + 1])))
        back_copy(side, step).start()

    def forward(step):
        right_copy(step, queries.at[step, 0:rows]).wait_recv()

        @pl.when(step < half - 1)
        def _():
            right_copy(step + 1, queries.at[step, 0:rows]).start()
            left_copy(step, queries.at[step, rows:2 * rows]).wait_recv()

        @pl.when(step < half - 2)
        def _():
            left_copy(step + 1, queries.at[step, rows:2 * rows]).start()

    forward(0)
    score_start()

    def first(j, _):
        score_tile(0, j)
        return 0

    lax.fori_loop(0, tiles, first, 0)
    score_end(0)

    def turn(step, _):
        forward(step + 1)
        score_start()
        weigh_start(step)

        def both(j, _):
            score_tile(step + 1, j)
            weigh_tile(step, j)
            return 0

        lax.fori_loop(0, tiles, both, 0)
        score_end(step + 1)

        @pl.when(step == near - 1)
        def _():
            pass_first(0, near - 1)
            pass_first(1, near - 1)

        @pl.when(step >= near)
        def _():
            pass_merged(0, half - 2 - step)
            pass_merged(1, half - 2 - step)

        return 0

    lax.fori_loop(0, half - 1, turn, 0)
    pass_first(1, half - 2)
    weigh_start(half - 1)

    def last(j, _):
        weigh_tile(half - 1, j)
        return 0

    lax.fori_loop(0, tiles, last, 0)
    pass_first(0, half - 1)
    result = local(half - 1, 1)
    for step in range(half - 3, near - 1, -1):
        pass_merged(1, step)
        pass_merged(0, step + 1)
    pass_merged(0, near)
    for step in (0, near):
        for side in (1, 0):
            back_copy(side, step).wait_recv()
            result = merge(result, unpack(landed.at[side, step]))
    out_ref[0] = (result[0] / result[1]).reshape(heads, tokens, width).astype(jnp.bfloat16)

    for step in range(half):
        right_copy(step, own).wait_send()
        back_copy(0, step).wait_send()
        if step < half - 1:
            left_copy(step, own).wait_send()
            back_copy(1, step).wait_send()
    for k in range(1, groups):
        fresh_copy(k).wait_send()


def per_device(queries, cache_keys, cache_values, cache_counts, new_keys, new_values, new_positions):
    levels = lax.axis_size("ctx")
    groups = lax.axis_size("qh")
    _, heads, tokens, width = queries.shape
    slots = cache_keys.shape[1]
    rows = heads * tokens
    half = levels // 2
    vmem = pl.BlockSpec(memory_space=pltpu.VMEM)
    anywhere = pl.BlockSpec(memory_space=pl.ANY)
    packed = rows + STATS
    dma = pltpu.SemaphoreType.DMA
    scratch = [
        pltpu.VMEM(queries.shape, queries.dtype),
        pltpu.VMEM(new_keys.shape, new_keys.dtype),
        pltpu.VMEM(new_values.shape, new_values.dtype),
        pltpu.SMEM(cache_counts.shape, cache_counts.dtype),
        pltpu.SMEM(new_positions.shape, new_positions.dtype),
        pltpu.VMEM((slots, width), jnp.bfloat16),
        pltpu.VMEM((width, slots), jnp.bfloat16),
        pltpu.VMEM((slots, 2 * width), jnp.bfloat16),
        pltpu.VMEM((groups, 2 * STATS, width), jnp.bfloat16),
        pltpu.VMEM((LANES, width), jnp.bfloat16),
        pltpu.VMEM((LANES, 2 * width), jnp.bfloat16),
        pltpu.VMEM((2 * STATS, width), jnp.float32),
        pltpu.VMEM((levels * tokens, LANES), jnp.int32),
        pltpu.VMEM((8, LANES), jnp.int32),
        pltpu.VMEM((2, slots // TILE, 2 * rows, TILE), jnp.float32),
        pltpu.VMEM((2, 2 * rows, LANES), jnp.float32),
        pltpu.VMEM((2 * rows, LANES), jnp.float32),
        pltpu.VMEM((half, 2 * rows, width), jnp.bfloat16),
        pltpu.VMEM((half, 2 * rows, 2 * width), jnp.float32),
        pltpu.VMEM((half, 2 * rows, LANES), jnp.float32),
        pltpu.VMEM((2, half, packed, width), jnp.bfloat16),
        pltpu.VMEM((2, half, packed, width), jnp.bfloat16),
        dma((7,)),
        dma((groups,)),
        dma((groups,)),
        dma((2, half)),
        dma((2, half)),
        dma((2, half)),
        dma((2, half)),
    ]
    return pl.pallas_call(
        functools.partial(kernel, levels, groups),
        out_shape=jax.ShapeDtypeStruct(queries.shape, queries.dtype),
        in_specs=[anywhere] * 7,
        out_specs=vmem,
        scratch_shapes=scratch,
        compiler_params=pltpu.CompilerParams(
            collective_id=0, has_side_effects=True, vmem_limit_bytes=60 * 1024 * 1024
        ),
        cost_estimate=pl.CostEstimate(
            flops=4 * levels * rows * slots * width,
            bytes_accessed=4 * slots * width,
            transcendentals=levels * rows * slots,
        ),
        name="ring_attention",
    )(queries, cache_keys, cache_values, cache_counts, new_keys, new_values, new_positions)


def solution(mesh):
    placed = (
        P("kv", "qh", "ctx", None),
        P("kv", "ctx", None),
        P("kv", "ctx", None),
        P("ctx"),
        P("kv", ("ctx", "qh"), None),
        P("kv", ("ctx", "qh"), None),
        P(),
    )
    return jax.shard_map(
        per_device,
        mesh=mesh,
        in_specs=placed,
        out_specs=P("kv", "qh", "ctx", None),
        check_vma=False,
    )
```

```python
import functools

import jax
import jax.numpy as jnp
from jax import lax
from jax.experimental import pallas as pl
from jax.experimental.pallas import tpu as pltpu
from jax.sharding import PartitionSpec as P

LOG2E = 1.4426950408889634
TILE = 1024
LANES = 128
STATS = 16


def contract(a, b, dims):
    return lax.dot_general(a, b, (dims, ((), ())), preferred_element_type=jnp.float32)


def kernel(
    levels, groups, q_hbm, k_hbm, v_hbm, count_hbm, nk_hbm, nv_hbm, pos_hbm, out_ref,
    q_ref, nk_ref, nv_ref, count_ref, pos_ref, loaded, keys, values, fresh, fresh_keys, fresh_values, wide, place_col, place_row,
    scores, extra, tops, queries, total, peaks,
    sent, landed,
    load_sem, fresh_send, fresh_recv, ag_send, ag_recv, back_send, back_recv,
):
    _, heads, tokens, width = q_ref.shape
    rows = heads * tokens
    slots = keys.shape[1]
    tiles = slots // TILE
    half = levels // 2
    near = half // 2
    quarters = 4
    own_new = nk_ref.shape[1]
    factor = LOG2E * width ** -0.5
    me = lax.axis_index("ctx")
    group = lax.axis_index("qh")

    def level(offset):
        return lax.rem(me + offset + levels, levels)

    def send(src, dst, send_sem, recv_sem, where):
        return pltpu.make_async_remote_copy(
            src_ref=src, dst_ref=dst, send_sem=send_sem, recv_sem=recv_sem,
            device_id=where, device_id_type=pl.DeviceIdType.MESH,
        )

    loads = [
        pltpu.make_async_copy(src, dst, load_sem.at[i])
        for i, (src, dst) in enumerate((
            (q_hbm, q_ref), (nk_hbm, nk_ref), (nv_hbm, nv_ref), (count_hbm, count_ref), (pos_hbm, pos_ref),
            (k_hbm.at[0], loaded), (v_hbm.at[0], values.at[:, 0:width]),
        ))
    ]
    for load in loads:
        load.start()

    barrier = pltpu.get_barrier_semaphore()
    partners = (1, -1, near + 1, -near - 1, near, -near, half - 1, 1 - half, half)
    for distance in partners:
        pl.semaphore_signal(barrier, inc=1, device_id={"ctx": level(distance)}, device_id_type=pl.DeviceIdType.MESH)
    for k in range(1, groups):
        pl.semaphore_signal(
            barrier, inc=1, device_id={"qh": lax.rem(group + k, groups)}, device_id_type=pl.DeviceIdType.MESH
        )

    for load in loads[:5]:
        load.wait()
    queries[near - 1, 3 * rows:4 * rows, :] = (
        q_ref[0].astype(jnp.float32).reshape(rows, width).astype(jnp.bfloat16)
    )
    wide[...] = jnp.zeros_like(wide)
    wide[0:own_new, :] = nk_ref[0].astype(jnp.float32)
    wide[STATS:STATS + own_new, :] = nv_ref[0].astype(jnp.float32)
    fresh[group] = wide[...].astype(jnp.bfloat16)

    def note_places(j, _):
        for i in range(tokens):
            place_col[pl.ds(j * tokens + i, 1), :] = jnp.full((1, LANES), pos_ref[j * tokens + i], jnp.int32)
        return 0

    lax.fori_loop(0, levels, note_places, 0)
    lane = lax.broadcasted_iota(jnp.int32, (8, LANES), 1)
    row = jnp.full((8, LANES), 1 << 30, jnp.int32)
    for g in range(groups):
        for i in range(own_new):
            place = pos_ref[me * tokens + g * own_new + i]
            row = jnp.where(lane == g * STATS + i, place, row)
    place_row[...] = row

    pl.semaphore_wait(barrier, len(partners) + groups - 1)

    own = queries.at[near - 1, 3 * rows:4 * rows]

    def part(quarter):
        return slice(quarter * rows, (quarter + 1) * rows)

    def query_copy(quarter, step, src, hop):
        return send(
            src, queries.at[step, part(quarter)], ag_send.at[quarter, step], ag_recv.at[quarter, step],
            {"ctx": level(hop if quarter % 2 == 0 else -hop)},
        )

    for quarter in range(quarters):
        query_copy(quarter, 0, own, near + 1 if quarter >= 2 else 1).start()

    def fresh_copy(k):
        return send(
            fresh.at[group], fresh.at[group], fresh_send.at[k], fresh_recv.at[group],
            {"qh": lax.rem(group + k, groups)},
        )

    def fresh_arrival(k):
        other = lax.rem(group + k, groups)
        return send(fresh.at[other], fresh.at[other], fresh_send.at[k], fresh_recv.at[other], {"qh": other})

    for k in range(1, groups):
        fresh_copy(k).start()

    count = count_ref[0]
    loads[5].wait()
    loads[6].wait()
    first_key = loaded[0:16, :].astype(jnp.float32)[0:1, :]
    chunk = 1024

    def prepare(j, _):
        base = pl.multiple_of(j * chunk, chunk)
        at = pl.ds(base, chunk)
        valid = lax.broadcasted_iota(jnp.int32, (chunk, width), 0) + base < count
        mass = jnp.where(valid, 1.0, 0.0).astype(jnp.bfloat16)
        values[at, width:2 * width] = mass
        values[at, 0:width] = values[at, 0:width] * mass
        chosen = jnp.where(valid, loaded[at, :].astype(jnp.float32), first_key)
        keys[:, at] = chosen.T.astype(jnp.bfloat16)
        return 0

    lax.fori_loop(0, slots // chunk, prepare, 0)

    fresh_keys[...] = jnp.zeros_like(fresh_keys)
    fresh_values[:, 0:width] = jnp.zeros((LANES, width), jnp.bfloat16)
    fresh_values[:, width:2 * width] = jnp.ones((LANES, width), jnp.bfloat16)
    for k in range(1, groups):
        fresh_arrival(k).wait_recv()
    for g in range(groups):
        fresh_keys[g * STATS:(g + 1) * STATS, :] = fresh[g, 0:STATS, :]
        fresh_values[g * STATS:(g + 1) * STATS, 0:width] = fresh[g, STATS:2 * STATS, :]

    def score_tile(step, j):
        at = pl.ds(pl.multiple_of(j * TILE, TILE), TILE)
        made = contract(queries[step], keys[:, at], ((1,), (0,)))
        scores[step % 2, j] = made
        top = tops[...]
        for g in range(TILE // LANES):
            top = jnp.maximum(top, made[:, g * LANES:(g + 1) * LANES])
        tops[...] = top

    def score_start():
        tops[...] = jnp.full(tops.shape, -1e30, jnp.float32)

    def score_end(step):
        made = contract(queries[step], fresh_keys[...], ((1,), (1,)))
        owners = (
            level(-(step + 1)), level(step + 1), level(-(step + near + 1)),
            jnp.where(step == near - 1, me, level(step + near + 1)),
        )

        def causal(owner, made):
            place = place_col[pl.ds(pl.multiple_of(owner * tokens, 8), tokens), :]
            place = jnp.concatenate([place] * heads, axis=0)
            limit = jnp.broadcast_to(place_row[0:1, :], place.shape)
            return jnp.where(limit <= place, made, -1e30)

        made = jnp.concatenate([causal(owners[q], made[part(q)]) for q in range(quarters)], axis=0)
        extra[step % 2] = made
        top = jnp.max(jnp.maximum(tops[...], made), axis=1, keepdims=True)
        top = top.astype(jnp.bfloat16).astype(jnp.float32)
        peaks[step] = jnp.broadcast_to(top, (quarters * rows, LANES))

    def weigh(made, peak):
        return [
            jnp.exp2(made[:, g * LANES:(g + 1) * LANES] * factor - peak)
            for g in range(made.shape[1] // LANES)
        ]

    def weigh_start(step):
        weight = weigh(extra[step % 2], peaks[step] * factor)[0].astype(jnp.bfloat16)
        total[step] = contract(weight, fresh_values[...], ((1,), (0,)))

    def weigh_tile(step, j):
        at = pl.ds(pl.multiple_of(j * TILE, TILE), TILE)
        weight = jnp.concatenate(weigh(scores[step % 2, j], peaks[step] * factor), axis=1).astype(jnp.bfloat16)
        total[step] += contract(weight, values[at, :], ((1,), (0,)))

    eye = lax.broadcasted_iota(jnp.int32, (rows, LANES), 0) == lax.broadcasted_iota(jnp.int32, (rows, LANES), 1)

    def pack(ref, summed):
        number, mass, peak = summed
        ref[0:rows, :] = number.astype(jnp.bfloat16)
        peak_row = jnp.sum(jnp.where(eye, peak, 0.0), axis=0, keepdims=True)
        mass_row = jnp.sum(jnp.where(eye, mass, 0.0), axis=0, keepdims=True)
        mass_high = mass_row.astype(jnp.bfloat16).astype(jnp.float32)
        line = lax.broadcasted_iota(jnp.int32, (STATS, LANES), 0)
        stats = jnp.where(
            line == 0, peak_row, jnp.where(line == 1, mass_high, jnp.where(line == 2, mass_row - mass_high, 0.0))
        )
        ref[rows:rows + STATS, :] = stats.astype(jnp.bfloat16)

    def unpack(ref):
        number = ref[0:rows, :].astype(jnp.float32)
        stats = ref[rows:rows + STATS, :].astype(jnp.float32)

        def column(line):
            spread = jnp.where(eye, jnp.broadcast_to(line, (rows, LANES)), 0.0)
            return jnp.broadcast_to(jnp.sum(spread, axis=1, keepdims=True), (rows, LANES))

        return number, column(stats[1:2, :] + stats[2:3, :]), column(stats[0:1, :])

    def local(step, quarter):
        at = part(quarter)
        return total[step, at, 0:width], total[step, at, width:2 * width], peaks[step, at, :]

    def merge(a, b):
        peak = jnp.maximum(a[2], b[2])
        wa = jnp.exp2((a[2] - peak) * factor)
        wb = jnp.exp2((b[2] - peak) * factor)
        return a[0] * wa + b[0] * wb, a[1] * wa + b[1] * wb, peak

    last_step = (near - 1, near - 1, near - 1, near - 2)
    furthest = (near, near, half, half - 1)

    def back_copy(quarter, step):
        hop = jnp.where(step == last_step[quarter], -furthest[quarter], 1)
        return send(
            sent.at[quarter, step], landed.at[quarter, step], back_send.at[quarter, step],
            back_recv.at[quarter, step], {"ctx": level(hop if quarter % 2 == 0 else -hop)},
        )

    def pass_first(quarter):
        pack(sent.at[quarter, 0], local(0, quarter))
        back_copy(quarter, 0).start()

    def pass_merged(quarter, step):
        back_copy(quarter, step - 1).wait_recv()
        pack(sent.at[quarter, step], merge(local(step, quarter), unpack(landed.at[quarter, step - 1])))
        back_copy(quarter, step).start()

    def arrive(quarter, step):
        query_copy(quarter, step, own, 1).wait_recv()

    def follow(quarter, step):
        query_copy(quarter, step + 1, queries.at[step, part(quarter)], 1).start()

    def forward(step):
        for quarter in (0, 1, 2):
            arrive(quarter, step)

            @pl.when(step < near - 1)
            def _():
                follow(quarter, step)

        @pl.when(step < near - 1)
        def _():
            arrive(3, step)

        @pl.when(step < near - 2)
        def _():
            follow(3, step)

    forward(0)
    score_start()

    def first(j, _):
        score_tile(0, j)
        return 0

    lax.fori_loop(0, tiles, first, 0)
    score_end(0)

    def turn(step, _):
        forward(step + 1)
        score_start()
        weigh_start(step)

        def both(j, _):
            score_tile(step + 1, j)
            weigh_tile(step, j)
            return 0

        lax.fori_loop(0, tiles, both, 0)
        score_end(step + 1)

        @pl.when(step == 0)
        def _():
            for quarter in range(quarters):
                pass_first(quarter)

        @pl.when(step > 0)
        def _():
            for quarter in range(quarters):
                pass_merged(quarter, step)

        return 0

    lax.fori_loop(0, near - 1, turn, 0)
    weigh_start(near - 1)

    def last(j, _):
        weigh_tile(near - 1, j)
        return 0

    lax.fori_loop(0, tiles, last, 0)
    for quarter in (2, 0, 1):
        pass_merged(quarter, near - 1)
    result = local(near - 1, 3)
    for quarter in (3, 0, 1, 2):
        back_copy(quarter, last_step[quarter]).wait_recv()
        result = merge(result, unpack(landed.at[quarter, last_step[quarter]]))
    out_ref[0] = (result[0] / result[1]).reshape(heads, tokens, width).astype(jnp.bfloat16)

    for quarter in range(quarters):
        for step in range(last_step[quarter] + 1):
            query_copy(quarter, step, own, 1).wait_send()
            back_copy(quarter, step).wait_send()
    for k in range(1, groups):
        fresh_copy(k).wait_send()


def per_device(queries, cache_keys, cache_values, cache_counts, new_keys, new_values, new_positions):
    levels = lax.axis_size("ctx")
    groups = lax.axis_size("qh")
    _, heads, tokens, width = queries.shape
    slots = cache_keys.shape[1]
    rows = heads * tokens
    near = levels // 4
    vmem = pl.BlockSpec(memory_space=pltpu.VMEM)
    anywhere = pl.BlockSpec(memory_space=pl.ANY)
    packed = rows + STATS
    dma = pltpu.SemaphoreType.DMA
    scratch = [
        pltpu.VMEM(queries.shape, queries.dtype),
        pltpu.VMEM(new_keys.shape, new_keys.dtype),
        pltpu.VMEM(new_values.shape, new_values.dtype),
        pltpu.SMEM(cache_counts.shape, cache_counts.dtype),
        pltpu.SMEM(new_positions.shape, new_positions.dtype),
        pltpu.VMEM((slots, width), jnp.bfloat16),
        pltpu.VMEM((width, slots), jnp.bfloat16),
        pltpu.VMEM((slots, 2 * width), jnp.bfloat16),
        pltpu.VMEM((groups, 2 * STATS, width), jnp.bfloat16),
        pltpu.VMEM((LANES, width), jnp.bfloat16),
        pltpu.VMEM((LANES, 2 * width), jnp.bfloat16),
        pltpu.VMEM((2 * STATS, width), jnp.float32),
        pltpu.VMEM((levels * tokens, LANES), jnp.int32),
        pltpu.VMEM((8, LANES), jnp.int32),
        pltpu.VMEM((2, slots // TILE, 4 * rows, TILE), jnp.float32),
        pltpu.VMEM((2, 4 * rows, LANES), jnp.float32),
        pltpu.VMEM((4 * rows, LANES), jnp.float32),
        pltpu.VMEM((near, 4 * rows, width), jnp.bfloat16),
        pltpu.VMEM((near, 4 * rows, 2 * width), jnp.float32),
        pltpu.VMEM((near, 4 * rows, LANES), jnp.float32),
        pltpu.VMEM((4, near, packed, width), jnp.bfloat16),
        pltpu.VMEM((4, near, packed, width), jnp.bfloat16),
        dma((7,)),
        dma((groups,)),
        dma((groups,)),
        dma((4, near)),
        dma((4, near)),
        dma((4, near)),
        dma((4, near)),
    ]
    return pl.pallas_call(
        functools.partial(kernel, levels, groups),
        out_shape=jax.ShapeDtypeStruct(queries.shape, queries.dtype),
        in_specs=[anywhere] * 7,
        out_specs=vmem,
        scratch_shapes=scratch,
        compiler_params=pltpu.CompilerParams(
            collective_id=0, has_side_effects=True, vmem_limit_bytes=60 * 1024 * 1024
        ),
        cost_estimate=pl.CostEstimate(
            flops=4 * levels * rows * slots * width,
            bytes_accessed=4 * slots * width,
            transcendentals=levels * rows * slots,
        ),
        name="ring_attention",
    )(queries, cache_keys, cache_values, cache_counts, new_keys, new_values, new_positions)


def solution(mesh):
    placed = (
        P("kv", "qh", "ctx", None),
        P("kv", "ctx", None),
        P("kv", "ctx", None),
        P("ctx"),
        P("kv", ("ctx", "qh"), None),
        P("kv", ("ctx", "qh"), None),
        P(),
    )
    return jax.shard_map(
        per_device,
        mesh=mesh,
        in_specs=placed,
        out_specs=P("kv", "qh", "ctx", None),
        check_vma=False,
    )
```

```python
import functools

import jax
import jax.numpy as jnp
from jax import lax
from jax.experimental import pallas as pl
from jax.experimental.pallas import tpu as pltpu
from jax.sharding import PartitionSpec as P

LOG2E = 1.4426950408889634
TILE = 1024
LANES = 128
STATS = 16


def contract(a, b, dims):
    return lax.dot_general(a, b, (dims, ((), ())), preferred_element_type=jnp.float32)


def kernel(
    levels, groups, q_hbm, k_hbm, v_hbm, count_hbm, nk_hbm, nv_hbm, pos_hbm, out_ref,
    q_ref, nk_ref, nv_ref, count_ref, pos_ref, loaded, keys, values, fresh, fresh_keys, fresh_values, wide, place_col, place_row,
    scores_even, scores_odd, extra, tops, queries, total, peaks,
    sent, landed,
    load_sem, fresh_send, fresh_recv, ag_send, ag_recv, back_send, back_recv,
):
    _, heads, tokens, width = q_ref.shape
    rows = heads * tokens
    slots = keys.shape[1]
    tiles = slots // TILE
    half = levels // 2
    near = half // 2
    quarters = 4
    own_new = nk_ref.shape[1]
    factor = LOG2E * width ** -0.5
    me = lax.axis_index("ctx")
    group = lax.axis_index("qh")

    def level(offset):
        return lax.rem(me + offset + levels, levels)

    def send(src, dst, send_sem, recv_sem, where):
        return pltpu.make_async_remote_copy(
            src_ref=src, dst_ref=dst, send_sem=send_sem, recv_sem=recv_sem,
            device_id=where, device_id_type=pl.DeviceIdType.MESH,
        )

    loads = [
        pltpu.make_async_copy(src, dst, load_sem.at[i])
        for i, (src, dst) in enumerate((
            (q_hbm, q_ref), (nk_hbm, nk_ref), (nv_hbm, nv_ref), (count_hbm, count_ref), (pos_hbm, pos_ref),
            (k_hbm.at[0], loaded), (v_hbm.at[0], values.at[:, 0:width]),
        ))
    ]
    for load in loads:
        load.start()

    barrier = pltpu.get_barrier_semaphore()
    partners = (1, -1, near + 1, -near - 1, near, -near, half - 1, 1 - half, half)
    for distance in partners:
        pl.semaphore_signal(barrier, inc=1, device_id={"ctx": level(distance)}, device_id_type=pl.DeviceIdType.MESH)
    for k in range(1, groups):
        pl.semaphore_signal(
            barrier, inc=1, device_id={"qh": lax.rem(group + k, groups)}, device_id_type=pl.DeviceIdType.MESH
        )

    for load in loads[:5]:
        load.wait()
    queries[near - 1, 3 * rows:4 * rows, :] = (
        q_ref[0].astype(jnp.float32).reshape(rows, width).astype(jnp.bfloat16)
    )
    wide[...] = jnp.zeros_like(wide)
    wide[0:own_new, :] = nk_ref[0].astype(jnp.float32)
    wide[STATS:STATS + own_new, :] = nv_ref[0].astype(jnp.float32)
    fresh[group] = wide[...].astype(jnp.bfloat16)

    def note_places(j, _):
        for i in range(tokens):
            place_col[pl.ds(j * tokens + i, 1), :] = jnp.full((1, LANES), pos_ref[j * tokens + i], jnp.int32)
        return 0

    lax.fori_loop(0, levels, note_places, 0)
    lane = lax.broadcasted_iota(jnp.int32, (8, LANES), 1)
    row = jnp.full((8, LANES), 1 << 30, jnp.int32)
    for g in range(groups):
        for i in range(own_new):
            place = pos_ref[me * tokens + g * own_new + i]
            row = jnp.where(lane == g * STATS + i, place, row)
    place_row[...] = row

    pl.semaphore_wait(barrier, len(partners) + groups - 1)

    own = queries.at[near - 1, 3 * rows:4 * rows]

    def part(quarter):
        return slice(quarter * rows, (quarter + 1) * rows)

    def query_copy(quarter, step, src, hop):
        return send(
            src, queries.at[step, part(quarter)], ag_send.at[quarter, step], ag_recv.at[quarter, step],
            {"ctx": level(hop if quarter % 2 == 0 else -hop)},
        )

    for quarter in range(quarters):
        query_copy(quarter, 0, own, near + 1 if quarter >= 2 else 1).start()

    def fresh_copy(k):
        return send(
            fresh.at[group], fresh.at[group], fresh_send.at[k], fresh_recv.at[group],
            {"qh": lax.rem(group + k, groups)},
        )

    def fresh_arrival(k):
        other = lax.rem(group + k, groups)
        return send(fresh.at[other], fresh.at[other], fresh_send.at[k], fresh_recv.at[other], {"qh": other})

    for k in range(1, groups):
        fresh_copy(k).start()

    count = count_ref[0]
    loads[5].wait()
    loads[6].wait()
    first_key = loaded[0:16, :].astype(jnp.float32)[0:1, :]
    chunk = 1024

    def prepare(j, _):
        base = pl.multiple_of(j * chunk, chunk)
        at = pl.ds(base, chunk)
        valid = lax.broadcasted_iota(jnp.int32, (chunk, width), 0) + base < count
        mass = jnp.where(valid, 1.0, 0.0).astype(jnp.bfloat16)
        values[at, width:2 * width] = mass
        values[at, 0:width] = values[at, 0:width] * mass
        chosen = jnp.where(valid, loaded[at, :].astype(jnp.float32), first_key)
        keys[:, at] = chosen.T.astype(jnp.bfloat16)
        return 0

    lax.fori_loop(0, slots // chunk, prepare, 0)

    fresh_keys[...] = jnp.zeros_like(fresh_keys)
    fresh_values[:, 0:width] = jnp.zeros((LANES, width), jnp.bfloat16)
    fresh_values[:, width:2 * width] = jnp.ones((LANES, width), jnp.bfloat16)
    for k in range(1, groups):
        fresh_arrival(k).wait_recv()
    for g in range(groups):
        fresh_keys[g * STATS:(g + 1) * STATS, :] = fresh[g, 0:STATS, :]
        fresh_values[g * STATS:(g + 1) * STATS, 0:width] = fresh[g, STATS:2 * STATS, :]

    scores = (scores_even, scores_odd)

    def score_tile(step, j):
        at = pl.ds(pl.multiple_of(j * TILE, TILE), TILE)
        made = contract(queries[step], keys[:, at], ((1,), (0,)))
        scores[step % 2][j] = made
        top = tops[...]
        for g in range(TILE // LANES):
            top = jnp.maximum(top, made[:, g * LANES:(g + 1) * LANES])
        tops[...] = top

    def score_start():
        tops[...] = jnp.full(tops.shape, -1e30, jnp.float32)

    def score_end(step):
        made = contract(queries[step], fresh_keys[...], ((1,), (1,)))
        owners = (
            level(-(step + 1)), level(step + 1), level(-(step + near + 1)),
            me if step == near - 1 else level(step + near + 1),
        )

        def causal(owner, made):
            place = place_col[pl.ds(pl.multiple_of(owner * tokens, 8), tokens), :]
            place = jnp.concatenate([place] * heads, axis=0)
            limit = jnp.broadcast_to(place_row[0:1, :], place.shape)
            return jnp.where(limit <= place, made, -1e30)

        made = jnp.concatenate([causal(owners[q], made[part(q)]) for q in range(quarters)], axis=0)
        extra[step % 2] = made
        top = jnp.max(jnp.maximum(tops[...], made), axis=1, keepdims=True)
        top = top.astype(jnp.bfloat16).astype(jnp.float32)
        peaks[step] = jnp.broadcast_to(top, (quarters * rows, LANES))

    def weigh(made, peak):
        return [
            jnp.exp2(made[:, g * LANES:(g + 1) * LANES] * factor - peak)
            for g in range(made.shape[1] // LANES)
        ]

    def weigh_start(step):
        weight = weigh(extra[step % 2], peaks[step] * factor)[0].astype(jnp.bfloat16)
        total[step] = contract(weight, fresh_values[...], ((1,), (0,)))

    def weigh_tile(step, j):
        at = pl.ds(pl.multiple_of(j * TILE, TILE), TILE)
        weight = jnp.concatenate(weigh(scores[step % 2][j], peaks[step] * factor), axis=1).astype(jnp.bfloat16)
        total[step] += contract(weight, values[at, :], ((1,), (0,)))

    eye = lax.broadcasted_iota(jnp.int32, (rows, LANES), 0) == lax.broadcasted_iota(jnp.int32, (rows, LANES), 1)

    def pack(ref, summed):
        number, mass, peak = summed
        ref[0:rows, :] = number.astype(jnp.bfloat16)
        peak_row = jnp.sum(jnp.where(eye, peak, 0.0), axis=0, keepdims=True)
        mass_row = jnp.sum(jnp.where(eye, mass, 0.0), axis=0, keepdims=True)
        mass_high = mass_row.astype(jnp.bfloat16).astype(jnp.float32)
        line = lax.broadcasted_iota(jnp.int32, (STATS, LANES), 0)
        stats = jnp.where(
            line == 0, peak_row, jnp.where(line == 1, mass_high, jnp.where(line == 2, mass_row - mass_high, 0.0))
        )
        ref[rows:rows + STATS, :] = stats.astype(jnp.bfloat16)

    def unpack(ref):
        number = ref[0:rows, :].astype(jnp.float32)
        stats = ref[rows:rows + STATS, :].astype(jnp.float32)

        def column(line):
            spread = jnp.where(eye, jnp.broadcast_to(line, (rows, LANES)), 0.0)
            return jnp.broadcast_to(jnp.sum(spread, axis=1, keepdims=True), (rows, LANES))

        return number, column(stats[1:2, :] + stats[2:3, :]), column(stats[0:1, :])

    def local(step, quarter):
        at = part(quarter)
        return total[step, at, 0:width], total[step, at, width:2 * width], peaks[step, at, :]

    def merge(a, b):
        peak = jnp.maximum(a[2], b[2])
        wa = jnp.exp2((a[2] - peak) * factor)
        wb = jnp.exp2((b[2] - peak) * factor)
        return a[0] * wa + b[0] * wb, a[1] * wa + b[1] * wb, peak

    last_step = (near - 1, near - 1, near - 1, near - 2)
    furthest = (near, near, half, half - 1)

    def back_copy(quarter, step):
        hop = -furthest[quarter] if step == last_step[quarter] else 1
        return send(
            sent.at[quarter, step], landed.at[quarter, step], back_send.at[quarter, step],
            back_recv.at[quarter, step], {"ctx": level(hop if quarter % 2 == 0 else -hop)},
        )

    def pass_first(quarter):
        pack(sent.at[quarter, 0], local(0, quarter))
        back_copy(quarter, 0).start()

    def pass_merged(quarter, step):
        back_copy(quarter, step - 1).wait_recv()
        pack(sent.at[quarter, step], merge(local(step, quarter), unpack(landed.at[quarter, step - 1])))
        back_copy(quarter, step).start()

    def arrive(quarter, step):
        query_copy(quarter, step, own, 1).wait_recv()

    def follow(quarter, step):
        query_copy(quarter, step + 1, queries.at[step, part(quarter)], 1).start()

    def forward(step):
        for quarter in range(quarters):
            if step <= last_step[quarter]:
                arrive(quarter, step)
            if step < last_step[quarter]:
                follow(quarter, step)

    forward(0)
    score_start()

    def first(j, _):
        score_tile(0, j)
        return 0

    lax.fori_loop(0, tiles, first, 0)
    score_end(0)

    for step in range(near - 1):
        forward(step + 1)
        score_start()
        weigh_start(step)

        def both(j, _):
            score_tile(step + 1, j)
            weigh_tile(step, j)
            return 0

        lax.fori_loop(0, tiles, both, 0)
        score_end(step + 1)
        for quarter in range(quarters):
            if step == 0:
                pass_first(quarter)
            else:
                pass_merged(quarter, step)

    weigh_start(near - 1)

    def last(j, _):
        weigh_tile(near - 1, j)
        return 0

    lax.fori_loop(0, tiles, last, 0)
    for quarter in (2, 0, 1):
        pass_merged(quarter, near - 1)
    result = local(near - 1, 3)
    for quarter in (3, 0, 1, 2):
        back_copy(quarter, last_step[quarter]).wait_recv()
        result = merge(result, unpack(landed.at[quarter, last_step[quarter]]))
    out_ref[0] = (result[0] / result[1]).reshape(heads, tokens, width).astype(jnp.bfloat16)

    for quarter in range(quarters):
        for step in range(last_step[quarter] + 1):
            query_copy(quarter, step, own, 1).wait_send()
            back_copy(quarter, step).wait_send()
    for k in range(1, groups):
        fresh_copy(k).wait_send()


def per_device(queries, cache_keys, cache_values, cache_counts, new_keys, new_values, new_positions):
    levels = lax.axis_size("ctx")
    groups = lax.axis_size("qh")
    _, heads, tokens, width = queries.shape
    slots = cache_keys.shape[1]
    rows = heads * tokens
    near = levels // 4
    vmem = pl.BlockSpec(memory_space=pltpu.VMEM)
    anywhere = pl.BlockSpec(memory_space=pl.ANY)
    packed = rows + STATS
    dma = pltpu.SemaphoreType.DMA
    scratch = [
        pltpu.VMEM(queries.shape, queries.dtype),
        pltpu.VMEM(new_keys.shape, new_keys.dtype),
        pltpu.VMEM(new_values.shape, new_values.dtype),
        pltpu.SMEM(cache_counts.shape, cache_counts.dtype),
        pltpu.SMEM(new_positions.shape, new_positions.dtype),
        pltpu.VMEM((slots, width), jnp.bfloat16),
        pltpu.VMEM((width, slots), jnp.bfloat16),
        pltpu.VMEM((slots, 2 * width), jnp.bfloat16),
        pltpu.VMEM((groups, 2 * STATS, width), jnp.bfloat16),
        pltpu.VMEM((LANES, width), jnp.bfloat16),
        pltpu.VMEM((LANES, 2 * width), jnp.bfloat16),
        pltpu.VMEM((2 * STATS, width), jnp.float32),
        pltpu.VMEM((levels * tokens, LANES), jnp.int32),
        pltpu.VMEM((8, LANES), jnp.int32),
        pltpu.VMEM((slots // TILE, 4 * rows, TILE), jnp.float32),
        pltpu.VMEM((slots // TILE, 4 * rows, TILE), jnp.float32),
        pltpu.VMEM((2, 4 * rows, LANES), jnp.float32),
        pltpu.VMEM((4 * rows, LANES), jnp.float32),
        pltpu.VMEM((near, 4 * rows, width), jnp.bfloat16),
        pltpu.VMEM((near, 4 * rows, 2 * width), jnp.float32),
        pltpu.VMEM((near, 4 * rows, LANES), jnp.float32),
        pltpu.VMEM((4, near, packed, width), jnp.bfloat16),
        pltpu.VMEM((4, near, packed, width), jnp.bfloat16),
        dma((7,)),
        dma((groups,)),
        dma((groups,)),
        dma((4, near)),
        dma((4, near)),
        dma((4, near)),
        dma((4, near)),
    ]
    return pl.pallas_call(
        functools.partial(kernel, levels, groups),
        out_shape=jax.ShapeDtypeStruct(queries.shape, queries.dtype),
        in_specs=[anywhere] * 7,
        out_specs=vmem,
        scratch_shapes=scratch,
        compiler_params=pltpu.CompilerParams(
            collective_id=0, has_side_effects=True, vmem_limit_bytes=60 * 1024 * 1024
        ),
        cost_estimate=pl.CostEstimate(
            flops=4 * levels * rows * slots * width,
            bytes_accessed=4 * slots * width,
            transcendentals=levels * rows * slots,
        ),
        name="ring_attention",
    )(queries, cache_keys, cache_values, cache_counts, new_keys, new_values, new_positions)


def solution(mesh):
    placed = (
        P("kv", "qh", "ctx", None),
        P("kv", "ctx", None),
        P("kv", "ctx", None),
        P("ctx"),
        P("kv", ("ctx", "qh"), None),
        P("kv", ("ctx", "qh"), None),
        P(),
    )
    return jax.shard_map(
        per_device,
        mesh=mesh,
        in_specs=placed,
        out_specs=P("kv", "qh", "ctx", None),
        check_vma=False,
    )
```

```python
import functools

import jax
import jax.numpy as jnp
from jax import lax
from jax.experimental import pallas as pl
from jax.experimental.pallas import tpu as pltpu
from jax.sharding import PartitionSpec as P

LOG2E = 1.4426950408889634
TILE = 1024
LANES = 128
STATS = 16


def contract(a, b, dims):
    return lax.dot_general(a, b, (dims, ((), ())), preferred_element_type=jnp.float32)


def kernel(
    levels, groups, q_hbm, k_hbm, v_hbm, count_hbm, nk_hbm, nv_hbm, pos_hbm, out_ref,
    q_ref, nk_ref, nv_ref, count_ref, pos_ref, loaded, keys, values, fresh, fresh_keys, fresh_values, wide, place_col, place_row,
    scores, extra, tops, queries, total, peaks,
    sent, landed,
    load_sem, fresh_send, fresh_recv, ag_send, ag_recv, back_send, back_recv,
):
    _, heads, tokens, width = q_ref.shape
    rows = heads * tokens
    slots = keys.shape[1]
    tiles = slots // TILE
    half = levels // 2
    near = half // 2
    quarters = 4
    own_new = nk_ref.shape[1]
    factor = LOG2E * width ** -0.5
    me = lax.axis_index("ctx")
    group = lax.axis_index("qh")

    def level(offset):
        return lax.rem(me + offset + levels, levels)

    def send(src, dst, send_sem, recv_sem, where):
        return pltpu.make_async_remote_copy(
            src_ref=src, dst_ref=dst, send_sem=send_sem, recv_sem=recv_sem,
            device_id=where, device_id_type=pl.DeviceIdType.MESH,
        )

    loads = [
        pltpu.make_async_copy(src, dst, load_sem.at[i])
        for i, (src, dst) in enumerate((
            (q_hbm, q_ref), (nk_hbm, nk_ref), (nv_hbm, nv_ref), (count_hbm, count_ref), (pos_hbm, pos_ref),
            (k_hbm.at[0], loaded), (v_hbm.at[0], values.at[:, 0:width]),
        ))
    ]
    for load in loads:
        load.start()

    barrier = pltpu.get_barrier_semaphore()
    partners = (1, -1, near + 1, -near - 1, near, -near, half - 1, 1 - half, half)
    for distance in partners:
        pl.semaphore_signal(barrier, inc=1, device_id={"ctx": level(distance)}, device_id_type=pl.DeviceIdType.MESH)
    for k in range(1, groups):
        pl.semaphore_signal(
            barrier, inc=1, device_id={"qh": lax.rem(group + k, groups)}, device_id_type=pl.DeviceIdType.MESH
        )

    loads[0].wait()
    queries[near - 1, 3 * rows:4 * rows, :] = (
        q_ref[0].astype(jnp.float32).reshape(rows, width).astype(jnp.bfloat16)
    )
    pl.semaphore_wait(barrier, len(partners) + groups - 1)

    own = queries.at[near - 1, 3 * rows:4 * rows]

    def part(quarter):
        return pl.ds(pl.multiple_of(quarter * rows, 32), rows)

    def query_copy(quarter, step, src, hop):
        return send(
            src, queries.at[step, part(quarter)], ag_send.at[quarter, step], ag_recv.at[quarter, step],
            {"ctx": level(hop * (1 - 2 * (quarter % 2)))},
        )

    for quarter in range(quarters):
        query_copy(quarter, 0, own, near + 1 if quarter >= 2 else 1).start()

    for load in loads[1:5]:
        load.wait()
    wide[...] = jnp.zeros_like(wide)
    wide[0:own_new, :] = nk_ref[0].astype(jnp.float32)
    wide[STATS:STATS + own_new, :] = nv_ref[0].astype(jnp.float32)
    fresh[group] = wide[...].astype(jnp.bfloat16)

    def fresh_copy(k):
        return send(
            fresh.at[group], fresh.at[group], fresh_send.at[k], fresh_recv.at[group],
            {"qh": lax.rem(group + k, groups)},
        )

    def fresh_arrival(k):
        other = lax.rem(group + k, groups)
        return send(fresh.at[other], fresh.at[other], fresh_send.at[k], fresh_recv.at[other], {"qh": other})

    for k in range(1, groups):
        fresh_copy(k).start()

    def note_places(j, _):
        for i in range(tokens):
            place_col[pl.ds(j * tokens + i, 1), :] = jnp.full((1, LANES), pos_ref[j * tokens + i], jnp.int32)
        return 0

    lax.fori_loop(0, levels, note_places, 0)
    lane = lax.broadcasted_iota(jnp.int32, (8, LANES), 1)
    row = jnp.full((8, LANES), 1 << 30, jnp.int32)
    for g in range(groups):
        for i in range(own_new):
            place = pos_ref[me * tokens + g * own_new + i]
            row = jnp.where(lane == g * STATS + i, place, row)
    place_row[...] = row

    count = count_ref[0]
    loads[5].wait()
    loads[6].wait()
    first_key = loaded[0:16, :].astype(jnp.float32)[0:1, :]
    chunk = 1024

    def prepare(j, _):
        base = pl.multiple_of(j * chunk, chunk)
        at = pl.ds(base, chunk)
        valid = lax.broadcasted_iota(jnp.int32, (chunk, width), 0) + base < count
        mass = jnp.where(valid, 1.0, 0.0).astype(jnp.bfloat16)
        values[at, width:2 * width] = mass
        values[at, 0:width] = values[at, 0:width] * mass
        chosen = jnp.where(valid, loaded[at, :].astype(jnp.float32), first_key)
        keys[:, at] = chosen.T.astype(jnp.bfloat16)
        return 0

    lax.fori_loop(0, slots // chunk, prepare, 0)

    fresh_keys[...] = jnp.zeros_like(fresh_keys)
    fresh_values[:, 0:width] = jnp.zeros((LANES, width), jnp.bfloat16)
    fresh_values[:, width:2 * width] = jnp.ones((LANES, width), jnp.bfloat16)
    for k in range(1, groups):
        fresh_arrival(k).wait_recv()
    for g in range(groups):
        fresh_keys[g * STATS:(g + 1) * STATS, :] = fresh[g, 0:STATS, :]
        fresh_values[g * STATS:(g + 1) * STATS, 0:width] = fresh[g, STATS:2 * STATS, :]

    def score_tile(step, j):
        at = pl.ds(pl.multiple_of(j * TILE, TILE), TILE)
        made = contract(queries[step], keys[:, at], ((1,), (0,)))
        scores[j] = made
        top = tops[...]
        for g in range(TILE // LANES):
            top = jnp.maximum(top, made[:, g * LANES:(g + 1) * LANES])
        tops[...] = top

    def score_start():
        tops[...] = jnp.full(tops.shape, -1e30, jnp.float32)

    def score_end(step):
        made = contract(queries[step], fresh_keys[...], ((1,), (1,)))
        owners = (
            level(-(step + 1)), level(step + 1), level(-(step + near + 1)),
            jnp.where(step == near - 1, me, level(step + near + 1)),
        )

        def causal(owner, made):
            place = place_col[pl.ds(pl.multiple_of(owner * tokens, 8), tokens), :]
            place = jnp.concatenate([place] * heads, axis=0)
            limit = jnp.broadcast_to(place_row[0:1, :], place.shape)
            return jnp.where(limit <= place, made, -1e30)

        made = jnp.concatenate([causal(owners[q], made[q * rows:(q + 1) * rows]) for q in range(quarters)], axis=0)
        extra[...] = made
        top = jnp.max(jnp.maximum(tops[...], made), axis=1, keepdims=True)
        top = top.astype(jnp.bfloat16).astype(jnp.float32)
        peaks[step] = jnp.broadcast_to(top, (quarters * rows, LANES))

    def weigh(made, peak):
        return [
            jnp.exp2(made[:, g * LANES:(g + 1) * LANES] * factor - peak)
            for g in range(made.shape[1] // LANES)
        ]

    def weigh_start(step):
        weight = weigh(extra[...], peaks[step] * factor)[0].astype(jnp.bfloat16)
        total[step] = contract(weight, fresh_values[...], ((1,), (0,)))

    def weigh_tile(step, j):
        at = pl.ds(pl.multiple_of(j * TILE, TILE), TILE)
        weight = jnp.concatenate(weigh(scores[j], peaks[step] * factor), axis=1).astype(jnp.bfloat16)
        total[step] += contract(weight, values[at, :], ((1,), (0,)))

    eye = lax.broadcasted_iota(jnp.int32, (rows, LANES), 0) == lax.broadcasted_iota(jnp.int32, (rows, LANES), 1)

    def pack(ref, summed):
        number, mass, peak = summed
        ref[0:rows, :] = number.astype(jnp.bfloat16)
        peak_row = jnp.sum(jnp.where(eye, peak, 0.0), axis=0, keepdims=True)
        mass_row = jnp.sum(jnp.where(eye, mass, 0.0), axis=0, keepdims=True)
        mass_high = mass_row.astype(jnp.bfloat16).astype(jnp.float32)
        line = lax.broadcasted_iota(jnp.int32, (STATS, LANES), 0)
        stats = jnp.where(
            line == 0, peak_row, jnp.where(line == 1, mass_high, jnp.where(line == 2, mass_row - mass_high, 0.0))
        )
        ref[rows:rows + STATS, :] = stats.astype(jnp.bfloat16)

    def unpack(ref):
        number = ref[0:rows, :].astype(jnp.float32)
        stats = ref[rows:rows + STATS, :].astype(jnp.float32)

        def column(line):
            spread = jnp.where(eye, jnp.broadcast_to(line, (rows, LANES)), 0.0)
            return jnp.broadcast_to(jnp.sum(spread, axis=1, keepdims=True), (rows, LANES))

        return number, column(stats[1:2, :] + stats[2:3, :]), column(stats[0:1, :])

    def local(step, quarter):
        at = part(quarter)
        return total[step, at, 0:width], total[step, at, width:2 * width], peaks[step, at, :]

    def merge(a, b):
        peak = jnp.maximum(a[2], b[2])
        wa = jnp.exp2((a[2] - peak) * factor)
        wb = jnp.exp2((b[2] - peak) * factor)
        return a[0] * wa + b[0] * wb, a[1] * wa + b[1] * wb, peak

    def last_step(quarter):
        return near - 1 - quarter // 3

    def back_copy(quarter, step):
        hop = jnp.where(step == last_step(quarter), -(near + near * (quarter // 2) - quarter // 3), 1)
        return send(
            sent.at[quarter, step], landed.at[quarter, step], back_send.at[quarter, step],
            back_recv.at[quarter, step], {"ctx": level(hop * (1 - 2 * (quarter % 2)))},
        )

    def pass_on(quarter, step):
        @pl.when(step > 0)
        def _():
            back_copy(quarter, step - 1).wait_recv()
            number, mass, peak = merge(local(step, quarter), unpack(landed.at[quarter, step - 1]))
            total[step, part(quarter), 0:width] = number
            total[step, part(quarter), width:2 * width] = mass
            peaks[step, part(quarter), :] = peak

        pack(sent.at[quarter, step], local(step, quarter))
        back_copy(quarter, step).start()

    def every(count, body):
        lax.fori_loop(0, count, lambda i, _: (body(i), 0)[1], 0)

    def forward(step):
        def one(quarter):
            @pl.when(step <= last_step(quarter))
            def _():
                query_copy(quarter, step, own, 1).wait_recv()

            @pl.when(step < last_step(quarter))
            def _():
                query_copy(quarter, step + 1, queries.at[step, part(quarter)], 1).start()

        every(quarters, one)

    forward(0)
    score_start()
    every(tiles, lambda j: score_tile(0, j))
    score_end(0)

    def turn(step):
        weigh_start(step)

        @pl.when(step < near - 1)
        def _():
            forward(step + 1)
            score_start()

            def both(j):
                weigh_tile(step, j)
                score_tile(step + 1, j)

            every(tiles, both)
            score_end(step + 1)

        @pl.when(step == near - 1)
        def _():
            every(tiles, lambda j: weigh_tile(step, j))

        def one(i):
            quarter = quarters - 1 - i

            @pl.when(step <= last_step(quarter))
            def _():
                pass_on(quarter, step)

        every(quarters, one)

    every(near, turn)
    result = local(near - 1, 3)
    for quarter in (3, 0, 1, 2):
        back_copy(quarter, last_step(quarter)).wait_recv()
        result = merge(result, unpack(landed.at[quarter, last_step(quarter)]))
    out_ref[0] = (result[0] / result[1]).reshape(heads, tokens, width).astype(jnp.bfloat16)

    def finish(i):
        quarter, step = i // near, i % near

        @pl.when(step <= last_step(quarter))
        def _():
            query_copy(quarter, step, own, 1).wait_send()
            back_copy(quarter, step).wait_send()

    every(quarters * near, finish)
    for k in range(1, groups):
        fresh_copy(k).wait_send()


def per_device(queries, cache_keys, cache_values, cache_counts, new_keys, new_values, new_positions):
    levels = lax.axis_size("ctx")
    groups = lax.axis_size("qh")
    _, heads, tokens, width = queries.shape
    slots = cache_keys.shape[1]
    rows = heads * tokens
    near = levels // 4
    vmem = pl.BlockSpec(memory_space=pltpu.VMEM)
    anywhere = pl.BlockSpec(memory_space=pl.ANY)
    packed = rows + STATS
    dma = pltpu.SemaphoreType.DMA
    scratch = [
        pltpu.VMEM(queries.shape, queries.dtype),
        pltpu.VMEM(new_keys.shape, new_keys.dtype),
        pltpu.VMEM(new_values.shape, new_values.dtype),
        pltpu.SMEM(cache_counts.shape, cache_counts.dtype),
        pltpu.SMEM(new_positions.shape, new_positions.dtype),
        pltpu.VMEM((slots, width), jnp.bfloat16),
        pltpu.VMEM((width, slots), jnp.bfloat16),
        pltpu.VMEM((slots, 2 * width), jnp.bfloat16),
        pltpu.VMEM((groups, 2 * STATS, width), jnp.bfloat16),
        pltpu.VMEM((LANES, width), jnp.bfloat16),
        pltpu.VMEM((LANES, 2 * width), jnp.bfloat16),
        pltpu.VMEM((2 * STATS, width), jnp.float32),
        pltpu.VMEM((levels * tokens, LANES), jnp.int32),
        pltpu.VMEM((8, LANES), jnp.int32),
        pltpu.VMEM((slots // TILE, 4 * rows, TILE), jnp.float32),
        pltpu.VMEM((4 * rows, LANES), jnp.float32),
        pltpu.VMEM((4 * rows, LANES), jnp.float32),
        pltpu.VMEM((near, 4 * rows, width), jnp.bfloat16),
        pltpu.VMEM((near, 4 * rows, 2 * width), jnp.float32),
        pltpu.VMEM((near, 4 * rows, LANES), jnp.float32),
        pltpu.VMEM((4, near, packed, width), jnp.bfloat16),
        pltpu.VMEM((4, near, packed, width), jnp.bfloat16),
        dma((7,)),
        dma((groups,)),
        dma((groups,)),
        dma((4, near)),
        dma((4, near)),
        dma((4, near)),
        dma((4, near)),
    ]
    return pl.pallas_call(
        functools.partial(kernel, levels, groups),
        out_shape=jax.ShapeDtypeStruct(queries.shape, queries.dtype),
        in_specs=[anywhere] * 7,
        out_specs=vmem,
        scratch_shapes=scratch,
        compiler_params=pltpu.CompilerParams(
            collective_id=0, has_side_effects=True, vmem_limit_bytes=60 * 1024 * 1024
        ),
        cost_estimate=pl.CostEstimate(
            flops=4 * levels * rows * slots * width,
            bytes_accessed=4 * slots * width,
            transcendentals=levels * rows * slots,
        ),
        name="ring_attention",
    )(queries, cache_keys, cache_values, cache_counts, new_keys, new_values, new_positions)


def solution(mesh):
    placed = (
        P("kv", "qh", "ctx", None),
        P("kv", "ctx", None),
        P("kv", "ctx", None),
        P("ctx"),
        P("kv", ("ctx", "qh"), None),
        P("kv", ("ctx", "qh"), None),
        P(),
    )
    return jax.shard_map(
        per_device,
        mesh=mesh,
        in_specs=placed,
        out_specs=P("kv", "qh", "ctx", None),
        check_vma=False,
    )
```

```python
import functools

import jax
import jax.numpy as jnp
from jax import lax
from jax.experimental import pallas as pl
from jax.experimental.pallas import tpu as pltpu
from jax.sharding import PartitionSpec as P

LOG2E = 1.4426950408889634
TILE = 2048
LANES = 128
STATS = 16


def contract(a, b, dims):
    return lax.dot_general(a, b, (dims, ((), ())), preferred_element_type=jnp.float32)


def kernel(
    levels, groups, q_hbm, k_hbm, v_hbm, count_hbm, nk_hbm, nv_hbm, pos_hbm, out_ref,
    q_ref, nk_ref, nv_ref, count_ref, pos_ref, loaded, keys, values, fresh, fresh_keys, fresh_values, wide, place_col, place_row,
    scores, extra, tops, queries, total, peaks,
    sent, landed,
    load_sem, fresh_send, fresh_recv, ag_send, ag_recv, back_send, back_recv,
):
    _, heads, tokens, width = q_ref.shape
    rows = heads * tokens
    slots = keys.shape[1]
    tiles = slots // TILE
    half = levels // 2
    near = half // 2
    sides = 2
    own_new = nk_ref.shape[1]
    factor = LOG2E * width ** -0.5
    me = lax.axis_index("ctx")
    group = lax.axis_index("qh")

    def level(offset):
        return lax.rem(me + offset + levels, levels)

    def send(src, dst, send_sem, recv_sem, where):
        return pltpu.make_async_remote_copy(
            src_ref=src, dst_ref=dst, send_sem=send_sem, recv_sem=recv_sem,
            device_id=where, device_id_type=pl.DeviceIdType.MESH,
        )

    loads = [
        pltpu.make_async_copy(src, dst, load_sem.at[i])
        for i, (src, dst) in enumerate((
            (q_hbm, q_ref), (nk_hbm, nk_ref), (nv_hbm, nv_ref), (count_hbm, count_ref), (pos_hbm, pos_ref),
            (k_hbm.at[0], loaded), (v_hbm.at[0], values.at[:, 0:width]),
        ))
    ]
    for load in loads:
        load.start()

    barrier = pltpu.get_barrier_semaphore()
    partners = (1, -1, near + 1, -near - 1)
    for distance in partners:
        pl.semaphore_signal(barrier, inc=1, device_id={"ctx": level(distance)}, device_id_type=pl.DeviceIdType.MESH)
    for k in range(1, groups):
        pl.semaphore_signal(
            barrier, inc=1, device_id={"qh": lax.rem(group + k, groups)}, device_id_type=pl.DeviceIdType.MESH
        )

    loads[0].wait()
    queries[half - 1, rows:2 * rows, :] = (
        q_ref[0].astype(jnp.float32).reshape(rows, width).astype(jnp.bfloat16)
    )
    pl.semaphore_wait(barrier, len(partners) + groups - 1)

    own = queries.at[half - 1, rows:2 * rows]

    def part(side):
        return pl.ds(pl.multiple_of(side * rows, 32), rows)

    def query_copy(side, step, src):
        return send(
            src, queries.at[step, part(side)], ag_send.at[side, step], ag_recv.at[side, step],
            {"ctx": level(1 - 2 * side)},
        )

    for side in range(sides):
        query_copy(side, 0, own).start()

    for load in loads[1:5]:
        load.wait()
    wide[...] = jnp.zeros_like(wide)
    wide[0:own_new, :] = nk_ref[0].astype(jnp.float32)
    wide[STATS:STATS + own_new, :] = nv_ref[0].astype(jnp.float32)
    fresh[group] = wide[...].astype(jnp.bfloat16)

    def fresh_copy(k):
        return send(
            fresh.at[group], fresh.at[group], fresh_send.at[k], fresh_recv.at[group],
            {"qh": lax.rem(group + k, groups)},
        )

    def fresh_arrival(k):
        other = lax.rem(group + k, groups)
        return send(fresh.at[other], fresh.at[other], fresh_send.at[k], fresh_recv.at[other], {"qh": other})

    for k in range(1, groups):
        fresh_copy(k).start()

    def note_places(j, _):
        for i in range(tokens):
            place_col[pl.ds(j * tokens + i, 1), :] = jnp.full((1, LANES), pos_ref[j * tokens + i], jnp.int32)
        return 0

    lax.fori_loop(0, levels, note_places, 0)
    lane = lax.broadcasted_iota(jnp.int32, (8, LANES), 1)
    row = jnp.full((8, LANES), 1 << 30, jnp.int32)
    for g in range(groups):
        for i in range(own_new):
            place = pos_ref[me * tokens + g * own_new + i]
            row = jnp.where(lane == g * STATS + i, place, row)
    place_row[...] = row

    count = count_ref[0]
    loads[5].wait()
    loads[6].wait()
    first_key = loaded[0:16, :].astype(jnp.float32)[0:1, :]
    chunk = 1024

    def prepare(j, _):
        base = pl.multiple_of(j * chunk, chunk)
        at = pl.ds(base, chunk)
        valid = lax.broadcasted_iota(jnp.int32, (chunk, width), 0) + base < count
        mass = jnp.where(valid, 1.0, 0.0).astype(jnp.bfloat16)
        values[at, width:2 * width] = mass
        values[at, 0:width] = values[at, 0:width] * mass
        chosen = jnp.where(valid, loaded[at, :].astype(jnp.float32), first_key)
        keys[:, at] = chosen.T.astype(jnp.bfloat16)
        return 0

    lax.fori_loop(0, slots // chunk, prepare, 0)

    fresh_keys[...] = jnp.zeros_like(fresh_keys)
    fresh_values[:, 0:width] = jnp.zeros((LANES, width), jnp.bfloat16)
    fresh_values[:, width:2 * width] = jnp.ones((LANES, width), jnp.bfloat16)
    for k in range(1, groups):
        fresh_arrival(k).wait_recv()
    for g in range(groups):
        fresh_keys[g * STATS:(g + 1) * STATS, :] = fresh[g, 0:STATS, :]
        fresh_values[g * STATS:(g + 1) * STATS, 0:width] = fresh[g, STATS:2 * STATS, :]

    def score_tile(step, j):
        at = pl.ds(pl.multiple_of(j * TILE, TILE), TILE)
        made = contract(queries[step], keys[:, at], ((1,), (0,)))
        scores[j] = made
        top = tops[...]
        for g in range(TILE // LANES):
            top = jnp.maximum(top, made[:, g * LANES:(g + 1) * LANES])
        tops[...] = top

    def score_start():
        tops[...] = jnp.full(tops.shape, -1e30, jnp.float32)

    def score_end(step):
        made = contract(queries[step], fresh_keys[...], ((1,), (1,)))
        owners = (level(-(step + 1)), jnp.where(step == half - 1, me, level(step + 1)))

        def causal(owner, made):
            place = place_col[pl.ds(pl.multiple_of(owner * tokens, 8), tokens), :]
            place = jnp.concatenate([place] * heads, axis=0)
            limit = jnp.broadcast_to(place_row[0:1, :], place.shape)
            return jnp.where(limit <= place, made, -1e30)

        made = jnp.concatenate([causal(owners[i], made[i * rows:(i + 1) * rows]) for i in range(sides)], axis=0)
        extra[...] = made
        top = jnp.max(jnp.maximum(tops[...], made), axis=1, keepdims=True)
        top = top.astype(jnp.bfloat16).astype(jnp.float32)
        peaks[step] = jnp.broadcast_to(top, (sides * rows, LANES))

    def weigh(made, peak):
        return [
            jnp.exp2(made[:, g * LANES:(g + 1) * LANES] * factor - peak)
            for g in range(made.shape[1] // LANES)
        ]

    def weigh_start(step):
        weight = weigh(extra[...], peaks[step] * factor)[0].astype(jnp.bfloat16)
        total[step] = contract(weight, fresh_values[...], ((1,), (0,)))

    def weigh_tile(step, j):
        at = pl.ds(pl.multiple_of(j * TILE, TILE), TILE)
        weight = jnp.concatenate(weigh(scores[j], peaks[step] * factor), axis=1).astype(jnp.bfloat16)
        total[step] += contract(weight, values[at, :], ((1,), (0,)))

    eye = lax.broadcasted_iota(jnp.int32, (rows, LANES), 0) == lax.broadcasted_iota(jnp.int32, (rows, LANES), 1)

    def pack(ref, summed):
        number, mass, peak = summed
        ref[0:rows, :] = number.astype(jnp.bfloat16)
        peak_row = jnp.sum(jnp.where(eye, peak, 0.0), axis=0, keepdims=True)
        mass_row = jnp.sum(jnp.where(eye, mass, 0.0), axis=0, keepdims=True)
        mass_high = mass_row.astype(jnp.bfloat16).astype(jnp.float32)
        line = lax.broadcasted_iota(jnp.int32, (STATS, LANES), 0)
        stats = jnp.where(
            line == 0, peak_row, jnp.where(line == 1, mass_high, jnp.where(line == 2, mass_row - mass_high, 0.0))
        )
        ref[rows:rows + STATS, :] = stats.astype(jnp.bfloat16)

    def unpack(ref):
        number = ref[0:rows, :].astype(jnp.float32)
        stats = ref[rows:rows + STATS, :].astype(jnp.float32)

        def column(line):
            spread = jnp.where(eye, jnp.broadcast_to(line, (rows, LANES)), 0.0)
            return jnp.broadcast_to(jnp.sum(spread, axis=1, keepdims=True), (rows, LANES))

        return number, column(stats[1:2, :] + stats[2:3, :]), column(stats[0:1, :])

    def local(step, side):
        at = part(side)
        return total[step, at, 0:width], total[step, at, width:2 * width], peaks[step, at, :]

    def merge(a, b):
        peak = jnp.maximum(a[2], b[2])
        wa = jnp.exp2((a[2] - peak) * factor)
        wb = jnp.exp2((b[2] - peak) * factor)
        return a[0] * wa + b[0] * wb, a[1] * wa + b[1] * wb, peak

    def back_copy(side, step):
        hop = jnp.where(step == near, near + 1, 1)
        return send(
            sent.at[side, step], landed.at[side, step], back_send.at[side, step], back_recv.at[side, step],
            {"ctx": level(hop * (2 * side - 1))},
        )

    def pass_on(side, step, merged):
        @pl.when(merged)
        def _():
            back_copy(side, step + 1).wait_recv()
            number, mass, peak = merge(local(step, side), unpack(landed.at[side, step + 1]))
            total[step, part(side), 0:width] = number
            total[step, part(side), width:2 * width] = mass
            peaks[step, part(side), :] = peak

        pack(sent.at[side, step], local(step, side))
        back_copy(side, step).start()

    def every(count, body):
        lax.fori_loop(0, count, lambda i, _: (body(i), 0)[1], 0)

    def forward(step):
        def one(side):
            @pl.when(step + side < half)
            def _():
                query_copy(side, step, own).wait_recv()

            @pl.when(step + side < half - 1)
            def _():
                query_copy(side, step + 1, queries.at[step, part(side)]).start()

        every(sides, one)

    forward(0)
    score_start()
    every(tiles, lambda j: score_tile(0, j))
    score_end(0)

    def turn(step):
        weigh_start(step)

        @pl.when(step < half - 1)
        def _():
            forward(step + 1)
            score_start()

            def both(j):
                weigh_tile(step, j)
                score_tile(step + 1, j)

            every(tiles, both)
            score_end(step + 1)

        @pl.when(step == half - 1)
        def _():
            every(tiles, lambda j: weigh_tile(step, j))

        @pl.when(step >= half - 2)
        def _():
            pass_on(half - 1 - step, step, step < 0)

        @pl.when((step >= near - 1) & (step < half - 1))
        def _():
            every(sides, lambda side: pass_on(side, jnp.where(step < near, step, half - 2 - step), step >= near))

    every(half, turn)
    for side, step in ((1, half - 3), (0, half - 2), (1, half - 4), (0, half - 3), (0, half - 4)):
        pass_on(side, step, step >= 0)
    result = local(half - 1, 1)
    for side, step in ((0, 0), (1, 0), (1, near), (0, near)):
        back_copy(side, step).wait_recv()
        result = merge(result, unpack(landed.at[side, step]))
    out_ref[0] = (result[0] / result[1]).reshape(heads, tokens, width).astype(jnp.bfloat16)

    def finish(i):
        side, step = i // half, i % half

        @pl.when(step + side < half)
        def _():
            query_copy(side, step, own).wait_send()
            back_copy(side, step).wait_send()

    every(sides * half, finish)
    for k in range(1, groups):
        fresh_copy(k).wait_send()


def per_device(queries, cache_keys, cache_values, cache_counts, new_keys, new_values, new_positions):
    levels = lax.axis_size("ctx")
    groups = lax.axis_size("qh")
    _, heads, tokens, width = queries.shape
    slots = cache_keys.shape[1]
    rows = heads * tokens
    half = levels // 2
    vmem = pl.BlockSpec(memory_space=pltpu.VMEM)
    anywhere = pl.BlockSpec(memory_space=pl.ANY)
    packed = rows + STATS
    dma = pltpu.SemaphoreType.DMA
    scratch = [
        pltpu.VMEM(queries.shape, queries.dtype),
        pltpu.VMEM(new_keys.shape, new_keys.dtype),
        pltpu.VMEM(new_values.shape, new_values.dtype),
        pltpu.SMEM(cache_counts.shape, cache_counts.dtype),
        pltpu.SMEM(new_positions.shape, new_positions.dtype),
        pltpu.VMEM((slots, width), jnp.bfloat16),
        pltpu.VMEM((width, slots), jnp.bfloat16),
        pltpu.VMEM((slots, 2 * width), jnp.bfloat16),
        pltpu.VMEM((groups, 2 * STATS, width), jnp.bfloat16),
        pltpu.VMEM((LANES, width), jnp.bfloat16),
        pltpu.VMEM((LANES, 2 * width), jnp.bfloat16),
        pltpu.VMEM((2 * STATS, width), jnp.float32),
        pltpu.VMEM((levels * tokens, LANES), jnp.int32),
        pltpu.VMEM((8, LANES), jnp.int32),
        pltpu.VMEM((slots // TILE, 2 * rows, TILE), jnp.float32),
        pltpu.VMEM((2 * rows, LANES), jnp.float32),
        pltpu.VMEM((2 * rows, LANES), jnp.float32),
        pltpu.VMEM((half, 2 * rows, width), jnp.bfloat16),
        pltpu.VMEM((half, 2 * rows, 2 * width), jnp.float32),
        pltpu.VMEM((half, 2 * rows, LANES), jnp.float32),
        pltpu.VMEM((2, half, packed, width), jnp.bfloat16),
        pltpu.VMEM((2, half, packed, width), jnp.bfloat16),
        dma((7,)),
        dma((groups,)),
        dma((groups,)),
        dma((2, half)),
        dma((2, half)),
        dma((2, half)),
        dma((2, half)),
    ]
    return pl.pallas_call(
        functools.partial(kernel, levels, groups),
        out_shape=jax.ShapeDtypeStruct(queries.shape, queries.dtype),
        in_specs=[anywhere] * 7,
        out_specs=vmem,
        scratch_shapes=scratch,
        compiler_params=pltpu.CompilerParams(
            collective_id=0, has_side_effects=True, vmem_limit_bytes=60 * 1024 * 1024
        ),
        cost_estimate=pl.CostEstimate(
            flops=4 * levels * rows * slots * width,
            bytes_accessed=4 * slots * width,
            transcendentals=levels * rows * slots,
        ),
        name="ring_attention",
    )(queries, cache_keys, cache_values, cache_counts, new_keys, new_values, new_positions)


def solution(mesh):
    placed = (
        P("kv", "qh", "ctx", None),
        P("kv", "ctx", None),
        P("kv", "ctx", None),
        P("ctx"),
        P("kv", ("ctx", "qh"), None),
        P("kv", ("ctx", "qh"), None),
        P(),
    )
    return jax.shard_map(
        per_device,
        mesh=mesh,
        in_specs=placed,
        out_specs=P("kv", "qh", "ctx", None),
        check_vma=False,
    )
```

```python
import functools

import jax
import jax.numpy as jnp
from jax import lax
from jax.experimental import pallas as pl
from jax.experimental.pallas import tpu as pltpu
from jax.sharding import PartitionSpec as P

LOG2E = 1.4426950408889634
TILE = 1024
LANES = 128
STATS = 16


def contract(a, b, dims):
    return lax.dot_general(a, b, (dims, ((), ())), preferred_element_type=jnp.float32)


def kernel(
    levels, groups, q_hbm, k_hbm, v_hbm, count_hbm, nk_hbm, nv_hbm, pos_hbm, out_ref,
    q_ref, nk_ref, nv_ref, count_ref, pos_ref, loaded, keys, values, fresh, fresh_keys, fresh_values, wide, place_col, place_row,
    scores, extra, tops, queries, total, peaks,
    sent, landed,
    load_sem, fresh_send, fresh_recv, ag_send, ag_recv, back_send, back_recv,
):
    _, heads, tokens, width = q_ref.shape
    rows = heads * tokens
    slots = keys.shape[1]
    tiles = slots // TILE
    half = levels // 2
    near = half // 2
    quarters = 4
    own_new = nk_ref.shape[1]
    factor = LOG2E * width ** -0.5
    me = lax.axis_index("ctx")
    group = lax.axis_index("qh")

    def level(offset):
        return lax.rem(me + offset + levels, levels)

    def send(src, dst, send_sem, recv_sem, where):
        return pltpu.make_async_remote_copy(
            src_ref=src, dst_ref=dst, send_sem=send_sem, recv_sem=recv_sem,
            device_id=where, device_id_type=pl.DeviceIdType.MESH,
        )

    loads = [
        pltpu.make_async_copy(src, dst, load_sem.at[i])
        for i, (src, dst) in enumerate((
            (q_hbm, q_ref), (nk_hbm, nk_ref), (nv_hbm, nv_ref), (count_hbm, count_ref), (pos_hbm, pos_ref),
            (k_hbm.at[0], loaded), (v_hbm.at[0], values.at[:, 0:width]),
        ))
    ]
    for load in loads:
        load.start()

    barrier = pltpu.get_barrier_semaphore()
    partners = (1, -1, near + 1, -near - 1, near, -near, half - 1, 1 - half, half)
    for distance in partners:
        pl.semaphore_signal(barrier, inc=1, device_id={"ctx": level(distance)}, device_id_type=pl.DeviceIdType.MESH)
    for k in range(1, groups):
        pl.semaphore_signal(
            barrier, inc=1, device_id={"qh": lax.rem(group + k, groups)}, device_id_type=pl.DeviceIdType.MESH
        )

    loads[0].wait()
    queries[near - 1, 3 * rows:4 * rows, :] = (
        q_ref[0].astype(jnp.float32).reshape(rows, width).astype(jnp.bfloat16)
    )
    pl.semaphore_wait(barrier, len(partners) + groups - 1)

    own = queries.at[near - 1, 3 * rows:4 * rows]

    def part(quarter):
        return pl.ds(pl.multiple_of(quarter * rows, 32), rows)

    def query_copy(quarter, step, src, hop):
        return send(
            src, queries.at[step, part(quarter)], ag_send.at[quarter, step], ag_recv.at[quarter, step],
            {"ctx": level(hop * (1 - 2 * (quarter % 2)))},
        )

    for quarter in range(quarters):
        query_copy(quarter, 0, own, near + 1 if quarter >= 2 else 1).start()

    for load in loads[1:5]:
        load.wait()
    wide[...] = jnp.zeros_like(wide)
    wide[0:own_new, :] = nk_ref[0].astype(jnp.float32)
    wide[STATS:STATS + own_new, :] = nv_ref[0].astype(jnp.float32)
    fresh[group] = wide[...].astype(jnp.bfloat16)

    def fresh_copy(k):
        return send(
            fresh.at[group], fresh.at[group], fresh_send.at[k], fresh_recv.at[group],
            {"qh": lax.rem(group + k, groups)},
        )

    def fresh_arrival(k):
        other = lax.rem(group + k, groups)
        return send(fresh.at[other], fresh.at[other], fresh_send.at[k], fresh_recv.at[other], {"qh": other})

    for k in range(1, groups):
        fresh_copy(k).start()

    def note_places(j, _):
        for i in range(tokens):
            place_col[pl.ds(j * tokens + i, 1), :] = jnp.full((1, LANES), pos_ref[j * tokens + i], jnp.int32)
        return 0

    lax.fori_loop(0, levels, note_places, 0)
    lane = lax.broadcasted_iota(jnp.int32, (8, LANES), 1)
    row = jnp.full((8, LANES), 1 << 30, jnp.int32)
    for g in range(groups):
        for i in range(own_new):
            place = pos_ref[me * tokens + g * own_new + i]
            row = jnp.where(lane == g * STATS + i, place, row)
    place_row[...] = row

    count = count_ref[0]
    loads[5].wait()
    loads[6].wait()
    first_key = loaded[0:16, :].astype(jnp.float32)[0:1, :]
    chunk = 1024

    def prepare(j, _):
        base = pl.multiple_of(j * chunk, chunk)
        at = pl.ds(base, chunk)
        valid = lax.broadcasted_iota(jnp.int32, (chunk, width), 0) + base < count
        mass = jnp.where(valid, 1.0, 0.0).astype(jnp.bfloat16)
        values[at, width:2 * width] = mass
        values[at, 0:width] = values[at, 0:width] * mass
        chosen = jnp.where(valid, loaded[at, :].astype(jnp.float32), first_key)
        keys[:, at] = chosen.T.astype(jnp.bfloat16)
        return 0

    lax.fori_loop(0, slots // chunk, prepare, 0)

    fresh_keys[...] = jnp.zeros_like(fresh_keys)
    fresh_values[:, 0:width] = jnp.zeros((LANES, width), jnp.bfloat16)
    fresh_values[:, width:2 * width] = jnp.ones((LANES, width), jnp.bfloat16)
    for k in range(1, groups):
        fresh_arrival(k).wait_recv()
    for g in range(groups):
        fresh_keys[g * STATS:(g + 1) * STATS, :] = fresh[g, 0:STATS, :]
        fresh_values[g * STATS:(g + 1) * STATS, 0:width] = fresh[g, STATS:2 * STATS, :]

    def score_tile(step, j):
        at = pl.ds(pl.multiple_of(j * TILE, TILE), TILE)
        made = contract(queries[step], keys[:, at], ((1,), (0,)))
        scores[j] = made
        top = tops[...]
        for g in range(TILE // LANES):
            top = jnp.maximum(top, made[:, g * LANES:(g + 1) * LANES])
        tops[...] = top

    def score_start():
        tops[...] = jnp.full(tops.shape, -1e30, jnp.float32)

    def score_end(step):
        made = contract(queries[step], fresh_keys[...], ((1,), (1,)))
        owners = (
            level(-(step + 1)), level(step + 1), level(-(step + near + 1)),
            jnp.where(step == near - 1, me, level(step + near + 1)),
        )

        def causal(owner, made):
            place = place_col[pl.ds(pl.multiple_of(owner * tokens, 8), tokens), :]
            place = jnp.concatenate([place] * heads, axis=0)
            limit = jnp.broadcast_to(place_row[0:1, :], place.shape)
            return jnp.where(limit <= place, made, -1e30)

        made = jnp.concatenate([causal(owners[q], made[q * rows:(q + 1) * rows]) for q in range(quarters)], axis=0)
        extra[...] = made
        top = jnp.max(jnp.maximum(tops[...], made), axis=1, keepdims=True)
        top = top.astype(jnp.bfloat16).astype(jnp.float32)
        peaks[step] = jnp.broadcast_to(top, (quarters * rows, LANES))

    def weigh(made, peak):
        return [
            jnp.exp2(made[:, g * LANES:(g + 1) * LANES] * factor - peak)
            for g in range(made.shape[1] // LANES)
        ]

    def weigh_start(step):
        weight = weigh(extra[...], peaks[step] * factor)[0].astype(jnp.bfloat16)
        total[step] = contract(weight, fresh_values[...], ((1,), (0,)))

    def weigh_tile(step, j):
        at = pl.ds(pl.multiple_of(j * TILE, TILE), TILE)
        weight = jnp.concatenate(weigh(scores[j], peaks[step] * factor), axis=1).astype(jnp.bfloat16)
        total[step] += contract(weight, values[at, :], ((1,), (0,)))

    lanes = lax.broadcasted_iota(jnp.int32, (rows, LANES), 1)
    line = lax.broadcasted_iota(jnp.int32, (STATS, LANES), 0)
    pick = jnp.where(line == lax.broadcasted_iota(jnp.int32, (STATS, LANES), 1), 1.0, 0.0).astype(jnp.bfloat16)
    spread = jnp.concatenate(
        [jnp.where(line == 0, 1.0, 0.0), jnp.where((line == 1) | (line == 2), 1.0, 0.0)], axis=1
    ).astype(jnp.bfloat16)

    def pack(ref, summed):
        number, mass, peak = summed
        ref[0:rows, :] = number.astype(jnp.bfloat16)
        mass_high = mass.astype(jnp.bfloat16).astype(jnp.float32)
        column = jnp.where(
            lanes == 0, peak, jnp.where(lanes == 1, mass_high, jnp.where(lanes == 2, mass - mass_high, 0.0))
        )
        column = jnp.concatenate([column, jnp.zeros((LANES - rows, LANES), jnp.float32)], axis=0)
        ref[rows:rows + STATS, :] = contract(pick, column.astype(jnp.bfloat16), ((1,), (1,))).astype(jnp.bfloat16)

    def unpack(ref):
        both = contract(ref[rows:rows + STATS, :], spread, ((0,), (0,)))[0:rows]
        return ref[0:rows, :].astype(jnp.float32), both[:, width:2 * width], both[:, 0:width]

    def local(step, quarter):
        at = part(quarter)
        return total[step, at, 0:width], total[step, at, width:2 * width], peaks[step, at, :]

    def merge(a, b):
        peak = jnp.maximum(a[2], b[2])
        wa = jnp.exp2((a[2] - peak) * factor)
        wb = jnp.exp2((b[2] - peak) * factor)
        return a[0] * wa + b[0] * wb, a[1] * wa + b[1] * wb, peak

    def last_step(quarter):
        return near - 1 - quarter // 3

    def back_copy(quarter, step):
        hop = jnp.where(step == last_step(quarter), -(near + near * (quarter // 2) - quarter // 3), 1)
        return send(
            sent.at[quarter, step], landed.at[quarter, step], back_send.at[quarter, step],
            back_recv.at[quarter, step], {"ctx": level(hop * (1 - 2 * (quarter % 2)))},
        )

    def pass_on(step, chosen, merged):
        if merged:
            for quarter in chosen:
                back_copy(quarter, step - 1).wait_recv()
        for quarter in chosen:
            summed = local(step, quarter)
            if merged:
                summed = merge(summed, unpack(landed.at[quarter, step - 1]))
            pack(sent.at[quarter, step], summed)
        for quarter in chosen:
            back_copy(quarter, step).start()

    def every(count, body):
        lax.fori_loop(0, count, lambda i, _: (body(i), 0)[1], 0)

    def forward(step):
        def one(quarter):
            @pl.when(step <= last_step(quarter))
            def _():
                query_copy(quarter, step, own, 1).wait_recv()

            @pl.when(step < last_step(quarter))
            def _():
                query_copy(quarter, step + 1, queries.at[step, part(quarter)], 1).start()

        every(quarters, one)

    forward(0)
    score_start()
    every(tiles, lambda j: score_tile(0, j))
    score_end(0)

    def turn(step):
        weigh_start(step)

        @pl.when(step < near - 1)
        def _():
            forward(step + 1)
            score_start()

            def both(j):
                weigh_tile(step, j)
                score_tile(step + 1, j)

            every(tiles, both)
            score_end(step + 1)

        @pl.when(step == near - 1)
        def _():
            every(tiles, lambda j: weigh_tile(step, j))

        everyone = (2, 3, 0, 1)
        pl.when(step == 0)(lambda: pass_on(step, everyone, False))
        pl.when((step > 0) & (step < near - 1))(lambda: pass_on(step, everyone, True))

    every(near, turn)
    pass_on(near - 1, (2, 0, 1), True)
    for quarter in (3, 0, 1, 2):
        back_copy(quarter, last_step(quarter)).wait_recv()
    gathered = [local(near - 1, 3)] + [unpack(landed.at[quarter, last_step(quarter)]) for quarter in range(quarters)]
    peak = functools.reduce(jnp.maximum, [one[2] for one in gathered])
    shares = [jnp.exp2((one[2] - peak) * factor) for one in gathered]
    result = (
        sum(one[0] * share for one, share in zip(gathered, shares)),
        sum(one[1] * share for one, share in zip(gathered, shares)),
    )
    out_ref[0] = (result[0] / result[1]).reshape(heads, tokens, width).astype(jnp.bfloat16)

    def finish(i):
        quarter, step = i // near, i % near

        @pl.when(step <= last_step(quarter))
        def _():
            query_copy(quarter, step, own, 1).wait_send()
            back_copy(quarter, step).wait_send()

    every(quarters * near, finish)
    for k in range(1, groups):
        fresh_copy(k).wait_send()


def per_device(queries, cache_keys, cache_values, cache_counts, new_keys, new_values, new_positions):
    levels = lax.axis_size("ctx")
    groups = lax.axis_size("qh")
    _, heads, tokens, width = queries.shape
    slots = cache_keys.shape[1]
    rows = heads * tokens
    near = levels // 4
    vmem = pl.BlockSpec(memory_space=pltpu.VMEM)
    anywhere = pl.BlockSpec(memory_space=pl.ANY)
    packed = rows + STATS
    dma = pltpu.SemaphoreType.DMA
    scratch = [
        pltpu.VMEM(queries.shape, queries.dtype),
        pltpu.VMEM(new_keys.shape, new_keys.dtype),
        pltpu.VMEM(new_values.shape, new_values.dtype),
        pltpu.SMEM(cache_counts.shape, cache_counts.dtype),
        pltpu.SMEM(new_positions.shape, new_positions.dtype),
        pltpu.VMEM((slots, width), jnp.bfloat16),
        pltpu.VMEM((width, slots), jnp.bfloat16),
        pltpu.VMEM((slots, 2 * width), jnp.bfloat16),
        pltpu.VMEM((groups, 2 * STATS, width), jnp.bfloat16),
        pltpu.VMEM((LANES, width), jnp.bfloat16),
        pltpu.VMEM((LANES, 2 * width), jnp.bfloat16),
        pltpu.VMEM((2 * STATS, width), jnp.float32),
        pltpu.VMEM((levels * tokens, LANES), jnp.int32),
        pltpu.VMEM((8, LANES), jnp.int32),
        pltpu.VMEM((slots // TILE, 4 * rows, TILE), jnp.float32),
        pltpu.VMEM((4 * rows, LANES), jnp.float32),
        pltpu.VMEM((4 * rows, LANES), jnp.float32),
        pltpu.VMEM((near, 4 * rows, width), jnp.bfloat16),
        pltpu.VMEM((near, 4 * rows, 2 * width), jnp.float32),
        pltpu.VMEM((near, 4 * rows, LANES), jnp.float32),
        pltpu.VMEM((4, near, packed, width), jnp.bfloat16),
        pltpu.VMEM((4, near, packed, width), jnp.bfloat16),
        dma((7,)),
        dma((groups,)),
        dma((groups,)),
        dma((4, near)),
        dma((4, near)),
        dma((4, near)),
        dma((4, near)),
    ]
    return pl.pallas_call(
        functools.partial(kernel, levels, groups),
        out_shape=jax.ShapeDtypeStruct(queries.shape, queries.dtype),
        in_specs=[anywhere] * 7,
        out_specs=vmem,
        scratch_shapes=scratch,
        compiler_params=pltpu.CompilerParams(
            collective_id=0, has_side_effects=True, vmem_limit_bytes=60 * 1024 * 1024
        ),
        cost_estimate=pl.CostEstimate(
            flops=4 * levels * rows * slots * width,
            bytes_accessed=4 * slots * width,
            transcendentals=levels * rows * slots,
        ),
        name="ring_attention",
    )(queries, cache_keys, cache_values, cache_counts, new_keys, new_values, new_positions)


def solution(mesh):
    placed = (
        P("kv", "qh", "ctx", None),
        P("kv", "ctx", None),
        P("kv", "ctx", None),
        P("ctx"),
        P("kv", ("ctx", "qh"), None),
        P("kv", ("ctx", "qh"), None),
        P(),
    )
    return jax.shard_map(
        per_device,
        mesh=mesh,
        in_specs=placed,
        out_specs=P("kv", "qh", "ctx", None),
        check_vma=False,
    )
```

```python
import functools

import jax
import jax.numpy as jnp
from jax import lax
from jax.experimental import pallas as pl
from jax.experimental.pallas import tpu as pltpu
from jax.sharding import PartitionSpec as P

LOG2E = 1.4426950408889634
TILE = 1024
LANES = 128
STATS = 16


def contract(a, b, dims):
    return lax.dot_general(a, b, (dims, ((), ())), preferred_element_type=jnp.float32)


def kernel(
    levels, groups, q_hbm, k_hbm, v_hbm, count_hbm, nk_hbm, nv_hbm, pos_hbm, out_ref,
    q_ref, nk_ref, nv_ref, count_ref, pos_ref, loaded, keys, values, fresh, fresh_keys, fresh_values, wide, place_col, place_row,
    scores, extra, tops, queries, total, peaks,
    sent, landed,
    load_sem, fresh_send, fresh_recv, ag_send, ag_recv, back_send, back_recv,
):
    _, heads, tokens, width = q_ref.shape
    rows = heads * tokens
    slots = keys.shape[1]
    tiles = slots // TILE
    half = levels // 2
    near = half // 2
    members = ((0, 1, 4), (0, 1, 2)) + ((0, 1, 2, 3),) * (near - 2) + ((2, 3),)
    steps = len(members)
    streams = (0, 1, 2, 3)
    first_step = (0, 0, 1, 2)
    last_step = (near - 1, near - 1, near, near)
    sign = (1, -1, 1, -1)

    def distance(stream, step):
        return step + 1 if stream < 2 else half + 1 - step

    own_new = nk_ref.shape[1]
    factor = LOG2E * width ** -0.5
    me = lax.axis_index("ctx")
    group = lax.axis_index("qh")

    def level(offset):
        return lax.rem(me + offset + levels, levels)

    def send(src, dst, send_sem, recv_sem, where):
        return pltpu.make_async_remote_copy(
            src_ref=src, dst_ref=dst, send_sem=send_sem, recv_sem=recv_sem,
            device_id=where, device_id_type=pl.DeviceIdType.MESH,
        )

    loads = [
        pltpu.make_async_copy(src, dst, load_sem.at[i])
        for i, (src, dst) in enumerate((
            (q_hbm, q_ref), (nk_hbm, nk_ref), (nv_hbm, nv_ref), (count_hbm, count_ref), (pos_hbm, pos_ref),
            (k_hbm.at[0], loaded), (v_hbm.at[0], values.at[:, 0:width]),
        ))
    ]
    for load in loads:
        load.start()

    barrier = pltpu.get_barrier_semaphore()
    partners = (1, -1, near + 1, -near - 1, near, -near, half - 1, 1 - half, half)
    for hop in partners:
        pl.semaphore_signal(barrier, inc=1, device_id={"ctx": level(hop)}, device_id_type=pl.DeviceIdType.MESH)
    for k in range(1, groups):
        pl.semaphore_signal(
            barrier, inc=1, device_id={"qh": lax.rem(group + k, groups)}, device_id_type=pl.DeviceIdType.MESH
        )

    loads[0].wait()
    queries[0, 2 * rows:3 * rows, :] = (
        q_ref[0].astype(jnp.float32).reshape(rows, width).astype(jnp.bfloat16)
    )
    pl.semaphore_wait(barrier, len(partners) + groups - 1)

    own = queries.at[0, 2 * rows:3 * rows]

    def part(stream, step):
        at = members[step].index(stream)
        return slice(at * rows, (at + 1) * rows)

    def onward(stream):
        return sign[stream] if stream < 2 else -sign[stream]

    def query_copy(stream, step, src):
        enters = step == first_step[stream]
        hop = sign[stream] * distance(stream, step) if enters else onward(stream)
        return send(
            src, queries.at[step, part(stream, step)], ag_send.at[stream, step], ag_recv.at[stream, step],
            {"ctx": level(hop)},
        )

    for stream in streams:
        query_copy(stream, first_step[stream], own).start()

    for load in loads[1:5]:
        load.wait()
    wide[...] = jnp.zeros_like(wide)
    wide[0:own_new, :] = nk_ref[0].astype(jnp.float32)
    wide[STATS:STATS + own_new, :] = nv_ref[0].astype(jnp.float32)
    fresh[group] = wide[...].astype(jnp.bfloat16)

    def fresh_copy(k):
        return send(
            fresh.at[group], fresh.at[group], fresh_send.at[k], fresh_recv.at[group],
            {"qh": lax.rem(group + k, groups)},
        )

    def fresh_arrival(k):
        other = lax.rem(group + k, groups)
        return send(fresh.at[other], fresh.at[other], fresh_send.at[k], fresh_recv.at[other], {"qh": other})

    for k in range(1, groups):
        fresh_copy(k).start()

    def note_places(j, _):
        for i in range(tokens):
            place_col[pl.ds(j * tokens + i, 1), :] = jnp.full((1, LANES), pos_ref[j * tokens + i], jnp.int32)
        return 0

    lax.fori_loop(0, levels, note_places, 0)
    lane = lax.broadcasted_iota(jnp.int32, (8, LANES), 1)
    row = jnp.full((8, LANES), 1 << 30, jnp.int32)
    for g in range(groups):
        for i in range(own_new):
            place = pos_ref[me * tokens + g * own_new + i]
            row = jnp.where(lane == g * STATS + i, place, row)
    place_row[...] = row

    count = count_ref[0]
    loads[5].wait()
    loads[6].wait()
    first_key = loaded[0:16, :].astype(jnp.float32)[0:1, :]
    chunk = 1024

    def prepare(j, _):
        base = pl.multiple_of(j * chunk, chunk)
        at = pl.ds(base, chunk)
        valid = lax.broadcasted_iota(jnp.int32, (chunk, width), 0) + base < count
        mass = jnp.where(valid, 1.0, 0.0).astype(jnp.bfloat16)
        values[at, width:2 * width] = mass
        values[at, 0:width] = values[at, 0:width] * mass
        chosen = jnp.where(valid, loaded[at, :].astype(jnp.float32), first_key)
        keys[:, at] = chosen.T.astype(jnp.bfloat16)
        return 0

    lax.fori_loop(0, slots // chunk, prepare, 0)

    fresh_keys[...] = jnp.zeros_like(fresh_keys)
    fresh_values[:, 0:width] = jnp.zeros((LANES, width), jnp.bfloat16)
    fresh_values[:, width:2 * width] = jnp.ones((LANES, width), jnp.bfloat16)
    for k in range(1, groups):
        fresh_arrival(k).wait_recv()
    for g in range(groups):
        fresh_keys[g * STATS:(g + 1) * STATS, :] = fresh[g, 0:STATS, :]
        fresh_values[g * STATS:(g + 1) * STATS, 0:width] = fresh[g, STATS:2 * STATS, :]

    def height(step):
        return len(members[step]) * rows

    def score_tile(step, j):
        at = pl.ds(pl.multiple_of(j * TILE, TILE), TILE)
        here = slice(0, height(step))
        made = contract(queries[step, here], keys[:, at], ((1,), (0,)))
        scores[j, here] = made
        top = tops[here]
        for g in range(TILE // LANES):
            top = jnp.maximum(top, made[:, g * LANES:(g + 1) * LANES])
        tops[here] = top

    def score_start():
        tops[...] = jnp.full(tops.shape, -1e30, jnp.float32)

    def score_end(step):
        here = slice(0, height(step))
        made = contract(queries[step, here], fresh_keys[...], ((1,), (1,)))

        def causal(stream):
            owner = me if stream == 4 else level(-sign[stream] * distance(stream, step))
            scored = made[part(stream, step)]
            place = place_col[pl.ds(pl.multiple_of(owner * tokens, 8), tokens), :]
            place = jnp.concatenate([place] * heads, axis=0)
            limit = jnp.broadcast_to(place_row[0:1, :], place.shape)
            return jnp.where(limit <= place, scored, -1e30)

        masked = jnp.concatenate([causal(stream) for stream in members[step]], axis=0)
        extra[here] = masked
        top = jnp.max(jnp.maximum(tops[here], masked), axis=1, keepdims=True)
        top = top.astype(jnp.bfloat16).astype(jnp.float32)
        peaks[step, here] = jnp.broadcast_to(top, (height(step), LANES))

    def weigh(made, peak):
        return [
            jnp.exp2(made[:, g * LANES:(g + 1) * LANES] * factor - peak)
            for g in range(made.shape[1] // LANES)
        ]

    def weigh_start(step):
        here = slice(0, height(step))
        weight = weigh(extra[here], peaks[step, here] * factor)[0].astype(jnp.bfloat16)
        total[step, here] = contract(weight, fresh_values[...], ((1,), (0,)))

    def weigh_tile(step, j):
        at = pl.ds(pl.multiple_of(j * TILE, TILE), TILE)
        here = slice(0, height(step))
        weight = jnp.concatenate(weigh(scores[j, here], peaks[step, here] * factor), axis=1).astype(jnp.bfloat16)
        total[step, here] += contract(weight, values[at, :], ((1,), (0,)))

    eye = lax.broadcasted_iota(jnp.int32, (rows, LANES), 0) == lax.broadcasted_iota(jnp.int32, (rows, LANES), 1)

    def pack(ref, summed):
        number, mass, peak = summed
        ref[0:rows, :] = number.astype(jnp.bfloat16)
        peak_row = jnp.sum(jnp.where(eye, peak, 0.0), axis=0, keepdims=True)
        mass_row = jnp.sum(jnp.where(eye, mass, 0.0), axis=0, keepdims=True)
        mass_high = mass_row.astype(jnp.bfloat16).astype(jnp.float32)
        line = lax.broadcasted_iota(jnp.int32, (STATS, LANES), 0)
        stats = jnp.where(
            line == 0, peak_row, jnp.where(line == 1, mass_high, jnp.where(line == 2, mass_row - mass_high, 0.0))
        )
        ref[rows:rows + STATS, :] = stats.astype(jnp.bfloat16)

    def unpack(ref):
        number = ref[0:rows, :].astype(jnp.float32)
        stats = ref[rows:rows + STATS, :].astype(jnp.float32)

        def column(line):
            spread = jnp.where(eye, jnp.broadcast_to(line, (rows, LANES)), 0.0)
            return jnp.broadcast_to(jnp.sum(spread, axis=1, keepdims=True), (rows, LANES))

        return number, column(stats[1:2, :] + stats[2:3, :]), column(stats[0:1, :])

    def local(step, stream):
        at = part(stream, step)
        return total[step, at, 0:width], total[step, at, width:2 * width], peaks[step, at, :]

    def merge(a, b):
        peak = jnp.maximum(a[2], b[2])
        wa = jnp.exp2((a[2] - peak) * factor)
        wb = jnp.exp2((b[2] - peak) * factor)
        return a[0] * wa + b[0] * wb, a[1] * wa + b[1] * wb, peak

    def back_copy(stream, step):
        hop = -sign[stream] * distance(stream, step) if step == last_step[stream] else onward(stream)
        return send(
            sent.at[stream, step], landed.at[stream, step], back_send.at[stream, step], back_recv.at[stream, step],
            {"ctx": level(hop)},
        )

    def pass_on(stream, step):
        summed = local(step, stream)
        if step > first_step[stream]:
            back_copy(stream, step - 1).wait_recv()
            summed = merge(summed, unpack(landed.at[stream, step - 1]))
        pack(sent.at[stream, step], summed)
        back_copy(stream, step).start()

    def every(count, body):
        lax.fori_loop(0, count, lambda i, _: (body(i), 0)[1], 0)

    def forward(step):
        for stream in members[step]:
            if stream in streams:
                query_copy(stream, step, own).wait_recv()
                if step < last_step[stream]:
                    query_copy(stream, step + 1, queries.at[step, part(stream, step)]).start()

    forward(0)
    score_start()
    every(tiles, lambda j: score_tile(0, j))
    score_end(0)
    for step in range(steps):
        weigh_start(step)
        if step < steps - 1:
            forward(step + 1)
            score_start()

            def both(j):
                weigh_tile(step, j)
                score_tile(step + 1, j)

            every(tiles, both)
            score_end(step + 1)
        else:
            every(tiles, lambda j: weigh_tile(step, j))
        for stream in reversed(members[step]):
            if stream in streams:
                pass_on(stream, step)

    result = local(0, 4)
    for stream in streams:
        back_copy(stream, last_step[stream]).wait_recv()
        result = merge(result, unpack(landed.at[stream, last_step[stream]]))
    out_ref[0] = (result[0] / result[1]).reshape(heads, tokens, width).astype(jnp.bfloat16)

    for stream in streams:
        for step in range(first_step[stream], last_step[stream] + 1):
            query_copy(stream, step, own).wait_send()
            back_copy(stream, step).wait_send()
    for k in range(1, groups):
        fresh_copy(k).wait_send()


def per_device(queries, cache_keys, cache_values, cache_counts, new_keys, new_values, new_positions):
    levels = lax.axis_size("ctx")
    groups = lax.axis_size("qh")
    _, heads, tokens, width = queries.shape
    slots = cache_keys.shape[1]
    rows = heads * tokens
    near = levels // 4
    vmem = pl.BlockSpec(memory_space=pltpu.VMEM)
    anywhere = pl.BlockSpec(memory_space=pl.ANY)
    packed = rows + STATS
    dma = pltpu.SemaphoreType.DMA
    scratch = [
        pltpu.VMEM(queries.shape, queries.dtype),
        pltpu.VMEM(new_keys.shape, new_keys.dtype),
        pltpu.VMEM(new_values.shape, new_values.dtype),
        pltpu.SMEM(cache_counts.shape, cache_counts.dtype),
        pltpu.SMEM(new_positions.shape, new_positions.dtype),
        pltpu.VMEM((slots, width), jnp.bfloat16),
        pltpu.VMEM((width, slots), jnp.bfloat16),
        pltpu.VMEM((slots, 2 * width), jnp.bfloat16),
        pltpu.VMEM((groups, 2 * STATS, width), jnp.bfloat16),
        pltpu.VMEM((LANES, width), jnp.bfloat16),
        pltpu.VMEM((LANES, 2 * width), jnp.bfloat16),
        pltpu.VMEM((2 * STATS, width), jnp.float32),
        pltpu.VMEM((levels * tokens, LANES), jnp.int32),
        pltpu.VMEM((8, LANES), jnp.int32),
        pltpu.VMEM((slots // TILE, 4 * rows, TILE), jnp.float32),
        pltpu.VMEM((4 * rows, LANES), jnp.float32),
        pltpu.VMEM((4 * rows, LANES), jnp.float32),
        pltpu.VMEM((near + 1, 4 * rows, width), jnp.bfloat16),
        pltpu.VMEM((near + 1, 4 * rows, 2 * width), jnp.float32),
        pltpu.VMEM((near + 1, 4 * rows, LANES), jnp.float32),
        pltpu.VMEM((4, near + 1, packed, width), jnp.bfloat16),
        pltpu.VMEM((4, near + 1, packed, width), jnp.bfloat16),
        dma((7,)),
        dma((groups,)),
        dma((groups,)),
        dma((4, near + 1)),
        dma((4, near + 1)),
        dma((4, near + 1)),
        dma((4, near + 1)),
    ]
    return pl.pallas_call(
        functools.partial(kernel, levels, groups),
        out_shape=jax.ShapeDtypeStruct(queries.shape, queries.dtype),
        in_specs=[anywhere] * 7,
        out_specs=vmem,
        scratch_shapes=scratch,
        compiler_params=pltpu.CompilerParams(
            collective_id=0, has_side_effects=True, vmem_limit_bytes=60 * 1024 * 1024
        ),
        cost_estimate=pl.CostEstimate(
            flops=4 * levels * rows * slots * width,
            bytes_accessed=4 * slots * width,
            transcendentals=levels * rows * slots,
        ),
        name="ring_attention",
    )(queries, cache_keys, cache_values, cache_counts, new_keys, new_values, new_positions)


def solution(mesh):
    placed = (
        P("kv", "qh", "ctx", None),
        P("kv", "ctx", None),
        P("kv", "ctx", None),
        P("ctx"),
        P("kv", ("ctx", "qh"), None),
        P("kv", ("ctx", "qh"), None),
        P(),
    )
    return jax.shard_map(
        per_device,
        mesh=mesh,
        in_specs=placed,
        out_specs=P("kv", "qh", "ctx", None),
        check_vma=False,
    )
```

```python
import functools

import jax
import jax.numpy as jnp
from jax import lax
from jax.experimental import pallas as pl
from jax.experimental.pallas import tpu as pltpu
from jax.sharding import PartitionSpec as P

LOG2E = 1.4426950408889634
TILE = 2048
LANES = 128
STATS = 16


def contract(a, b, dims):
    return lax.dot_general(a, b, (dims, ((), ())), preferred_element_type=jnp.float32)


def kernel(
    levels, groups, q_hbm, k_hbm, v_hbm, count_hbm, nk_hbm, nv_hbm, pos_hbm, out_ref,
    q_ref, nk_ref, nv_ref, count_ref, pos_ref, loaded, keys, values, fresh, fresh_keys, fresh_values, wide, place_col, place_row,
    scores, extra, tops, queries, total, peaks,
    sent, landed,
    load_sem, fresh_send, fresh_recv, ag_send, ag_recv, back_send, back_recv,
):
    _, heads, tokens, width = q_ref.shape
    rows = heads * tokens
    slots = keys.shape[1]
    tiles = slots // TILE
    half = levels // 2
    near = half // 2
    members = ((0, 1, 4), (0, 1, 2)) + ((0, 1, 2, 3),) * (near - 2) + ((2, 3),)
    steps = len(members)
    streams = (0, 1, 2, 3)
    first_step = (0, 0, 1, 2)
    last_step = (near - 1, near - 1, near, near)
    sign = (1, -1, 1, -1)

    def distance(stream, step):
        return step + 1 if stream < 2 else half + 1 - step

    own_new = nk_ref.shape[1]
    factor = LOG2E * width ** -0.5
    me = lax.axis_index("ctx")
    group = lax.axis_index("qh")

    def level(offset):
        return lax.rem(me + offset + levels, levels)

    def send(src, dst, send_sem, recv_sem, where):
        return pltpu.make_async_remote_copy(
            src_ref=src, dst_ref=dst, send_sem=send_sem, recv_sem=recv_sem,
            device_id=where, device_id_type=pl.DeviceIdType.MESH,
        )

    loads = [
        pltpu.make_async_copy(src, dst, load_sem.at[i])
        for i, (src, dst) in enumerate((
            (q_hbm, q_ref), (nk_hbm, nk_ref), (nv_hbm, nv_ref), (count_hbm, count_ref), (pos_hbm, pos_ref),
            (k_hbm.at[0], loaded), (v_hbm.at[0], values.at[:, 0:width]),
        ))
    ]
    for load in loads:
        load.start()

    barrier = pltpu.get_barrier_semaphore()
    partners = (1, -1, near + 1, -near - 1, near, -near, half - 1, 1 - half, half)
    for hop in partners:
        pl.semaphore_signal(barrier, inc=1, device_id={"ctx": level(hop)}, device_id_type=pl.DeviceIdType.MESH)
    for k in range(1, groups):
        pl.semaphore_signal(
            barrier, inc=1, device_id={"qh": lax.rem(group + k, groups)}, device_id_type=pl.DeviceIdType.MESH
        )

    loads[0].wait()
    queries[0, 2 * rows:3 * rows, :] = (
        q_ref[0].astype(jnp.float32).reshape(rows, width).astype(jnp.bfloat16)
    )
    pl.semaphore_wait(barrier, len(partners) + groups - 1)

    own = queries.at[0, 2 * rows:3 * rows]

    def part(stream, step):
        at = members[step].index(stream)
        return slice(at * rows, (at + 1) * rows)

    def onward(stream):
        return sign[stream] if stream < 2 else -sign[stream]

    def query_copy(stream, step, src):
        enters = step == first_step[stream]
        hop = sign[stream] * distance(stream, step) if enters else onward(stream)
        return send(
            src, queries.at[step, part(stream, step)], ag_send.at[stream, step], ag_recv.at[stream, step],
            {"ctx": level(hop)},
        )

    for stream in streams:
        query_copy(stream, first_step[stream], own).start()

    for load in loads[1:5]:
        load.wait()
    wide[...] = jnp.zeros_like(wide)
    wide[0:own_new, :] = nk_ref[0].astype(jnp.float32)
    wide[STATS:STATS + own_new, :] = nv_ref[0].astype(jnp.float32)
    fresh[group] = wide[...].astype(jnp.bfloat16)

    def fresh_copy(k):
        return send(
            fresh.at[group], fresh.at[group], fresh_send.at[k], fresh_recv.at[group],
            {"qh": lax.rem(group + k, groups)},
        )

    def fresh_arrival(k):
        other = lax.rem(group + k, groups)
        return send(fresh.at[other], fresh.at[other], fresh_send.at[k], fresh_recv.at[other], {"qh": other})

    for k in range(1, groups):
        fresh_copy(k).start()

    def note_places(j, _):
        for i in range(tokens):
            place_col[pl.ds(j * tokens + i, 1), :] = jnp.full((1, LANES), pos_ref[j * tokens + i], jnp.int32)
        return 0

    lax.fori_loop(0, levels, note_places, 0)
    lane = lax.broadcasted_iota(jnp.int32, (8, LANES), 1)
    row = jnp.full((8, LANES), 1 << 30, jnp.int32)
    for g in range(groups):
        for i in range(own_new):
            place = pos_ref[me * tokens + g * own_new + i]
            row = jnp.where(lane == g * STATS + i, place, row)
    place_row[...] = row

    def forward(step):
        for stream in members[step]:
            if stream in streams:
                query_copy(stream, step, own).wait_recv()
                if step < last_step[stream]:
                    query_copy(stream, step + 1, queries.at[step, part(stream, step)]).start()

    count = count_ref[0]
    loads[5].wait()
    loads[6].wait()
    first_key = loaded[0:16, :].astype(jnp.float32)[0:1, :]
    chunk = 1024 if slots % 2048 == 0 else 512

    def prepare(j, _):
        base = pl.multiple_of(j * chunk, chunk)
        at = pl.ds(base, chunk)
        valid = lax.broadcasted_iota(jnp.int32, (chunk, width), 0) + base < count
        mass = jnp.where(valid, 1.0, 0.0).astype(jnp.bfloat16)
        values[at, width:2 * width] = mass
        values[at, 0:width] = values[at, 0:width] * mass
        chosen = jnp.where(valid, loaded[at, :].astype(jnp.float32), first_key)
        keys[:, at] = chosen.astype(jnp.bfloat16).T
        return 0

    lax.fori_loop(0, slots // chunk // 2, prepare, 0)
    forward(0)
    lax.fori_loop(slots // chunk // 2, slots // chunk, prepare, 0)

    fresh_keys[...] = jnp.zeros_like(fresh_keys)
    fresh_values[:, 0:width] = jnp.zeros((LANES, width), jnp.bfloat16)
    fresh_values[:, width:2 * width] = jnp.ones((LANES, width), jnp.bfloat16)
    for k in range(1, groups):
        fresh_arrival(k).wait_recv()
    for g in range(groups):
        fresh_keys[g * STATS:(g + 1) * STATS, :] = fresh[g, 0:STATS, :]
        fresh_values[g * STATS:(g + 1) * STATS, 0:width] = fresh[g, STATS:2 * STATS, :]

    def height(step):
        return len(members[step]) * rows

    def score_tile(step, j):
        at = pl.ds(pl.multiple_of(j * TILE, TILE), TILE)
        here = slice(0, height(step))
        made = contract(queries[step, here], keys[:, at], ((1,), (0,)))
        scores[j, here] = made
        top = tops[here]
        for g in range(TILE // LANES):
            top = jnp.maximum(top, made[:, g * LANES:(g + 1) * LANES])
        tops[here] = top

    def score_start():
        tops[...] = jnp.full(tops.shape, -1e30, jnp.float32)

    def score_end(step):
        here = slice(0, height(step))
        made = contract(queries[step, here], fresh_keys[...], ((1,), (1,)))

        def causal(stream):
            owner = me if stream == 4 else level(-sign[stream] * distance(stream, step))
            scored = made[part(stream, step)]
            place = place_col[pl.ds(pl.multiple_of(owner * tokens, 8), tokens), :]
            place = jnp.concatenate([place] * heads, axis=0)
            limit = jnp.broadcast_to(place_row[0:1, :], place.shape)
            return jnp.where(limit <= place, scored, -1e30)

        masked = jnp.concatenate([causal(stream) for stream in members[step]], axis=0)
        extra[here] = masked
        top = jnp.max(jnp.maximum(tops[here], masked), axis=1, keepdims=True)
        top = top.astype(jnp.bfloat16).astype(jnp.float32)
        peaks[step, here] = jnp.broadcast_to(top, (height(step), LANES))

    def weigh(made, peak):
        return [
            jnp.exp2(made[:, g * LANES:(g + 1) * LANES] * factor - peak)
            for g in range(made.shape[1] // LANES)
        ]

    def weigh_start(step):
        here = slice(0, height(step))
        weight = weigh(extra[here], peaks[step, here] * factor)[0].astype(jnp.bfloat16)
        total[step, here] = contract(weight, fresh_values[...], ((1,), (0,)))

    def weigh_tile(step, j):
        at = pl.ds(pl.multiple_of(j * TILE, TILE), TILE)
        here = slice(0, height(step))
        weight = jnp.concatenate(weigh(scores[j, here], peaks[step, here] * factor), axis=1).astype(jnp.bfloat16)
        total[step, here] += contract(weight, values[at, :], ((1,), (0,)))

    eye = lax.broadcasted_iota(jnp.int32, (rows, LANES), 0) == lax.broadcasted_iota(jnp.int32, (rows, LANES), 1)

    def pack(ref, summed):
        number, mass, peak = summed
        ref[0:rows, :] = number.astype(jnp.bfloat16)
        peak_row = jnp.sum(jnp.where(eye, peak, 0.0), axis=0, keepdims=True)
        mass_row = jnp.sum(jnp.where(eye, mass, 0.0), axis=0, keepdims=True)
        mass_high = mass_row.astype(jnp.bfloat16).astype(jnp.float32)
        line = lax.broadcasted_iota(jnp.int32, (STATS, LANES), 0)
        stats = jnp.where(
            line == 0, peak_row, jnp.where(line == 1, mass_high, jnp.where(line == 2, mass_row - mass_high, 0.0))
        )
        ref[rows:rows + STATS, :] = stats.astype(jnp.bfloat16)

    def unpack(ref):
        number = ref[0:rows, :].astype(jnp.float32)
        stats = ref[rows:rows + STATS, :].astype(jnp.float32)

        def column(line):
            spread = jnp.where(eye, jnp.broadcast_to(line, (rows, LANES)), 0.0)
            return jnp.broadcast_to(jnp.sum(spread, axis=1, keepdims=True), (rows, LANES))

        return number, column(stats[1:2, :] + stats[2:3, :]), column(stats[0:1, :])

    def local(step, stream):
        at = part(stream, step)
        return total[step, at, 0:width], total[step, at, width:2 * width], peaks[step, at, :]

    def merge(a, b):
        peak = jnp.maximum(a[2], b[2])
        wa = jnp.exp2((a[2] - peak) * factor)
        wb = jnp.exp2((b[2] - peak) * factor)
        return a[0] * wa + b[0] * wb, a[1] * wa + b[1] * wb, peak

    def back_copy(stream, step):
        hop = -sign[stream] * distance(stream, step) if step == last_step[stream] else onward(stream)
        return send(
            sent.at[stream, step], landed.at[stream, step], back_send.at[stream, step], back_recv.at[stream, step],
            {"ctx": level(hop)},
        )

    def pass_on(stream, step):
        summed = local(step, stream)
        if step > first_step[stream]:
            back_copy(stream, step - 1).wait_recv()
            summed = merge(summed, unpack(landed.at[stream, step - 1]))
        pack(sent.at[stream, step], summed)
        back_copy(stream, step).start()

    def every(count, body):
        lax.fori_loop(0, count, lambda i, _: (body(i), 0)[1], 0)

    score_start()
    every(tiles, lambda j: score_tile(0, j))
    score_end(0)
    for step in range(steps):
        weigh_start(step)
        if step < steps - 1:
            forward(step + 1)
            score_start()

            def both(j):
                weigh_tile(step, j)
                score_tile(step + 1, j)

            every(tiles, both)
            score_end(step + 1)
        else:
            every(tiles, lambda j: weigh_tile(step, j))
        for stream in reversed(members[step]):
            if stream in streams:
                pass_on(stream, step)

    result = local(0, 4)
    for stream in streams:
        back_copy(stream, last_step[stream]).wait_recv()
        result = merge(result, unpack(landed.at[stream, last_step[stream]]))
    out_ref[0] = (result[0] / result[1]).reshape(heads, tokens, width).astype(jnp.bfloat16)

    for stream in streams:
        for step in range(first_step[stream], last_step[stream] + 1):
            query_copy(stream, step, own).wait_send()
            back_copy(stream, step).wait_send()
    for k in range(1, groups):
        fresh_copy(k).wait_send()


def per_device(queries, cache_keys, cache_values, cache_counts, new_keys, new_values, new_positions):
    levels = lax.axis_size("ctx")
    groups = lax.axis_size("qh")
    _, heads, tokens, width = queries.shape
    slots = cache_keys.shape[1]
    rows = heads * tokens
    near = levels // 4
    vmem = pl.BlockSpec(memory_space=pltpu.VMEM)
    anywhere = pl.BlockSpec(memory_space=pl.ANY)
    packed = rows + STATS
    dma = pltpu.SemaphoreType.DMA
    scratch = [
        pltpu.VMEM(queries.shape, queries.dtype),
        pltpu.VMEM(new_keys.shape, new_keys.dtype),
        pltpu.VMEM(new_values.shape, new_values.dtype),
        pltpu.SMEM(cache_counts.shape, cache_counts.dtype),
        pltpu.SMEM(new_positions.shape, new_positions.dtype),
        pltpu.VMEM((slots, width), jnp.bfloat16),
        pltpu.VMEM((width, slots), jnp.bfloat16),
        pltpu.VMEM((slots, 2 * width), jnp.bfloat16),
        pltpu.VMEM((groups, 2 * STATS, width), jnp.bfloat16),
        pltpu.VMEM((LANES, width), jnp.bfloat16),
        pltpu.VMEM((LANES, 2 * width), jnp.bfloat16),
        pltpu.VMEM((2 * STATS, width), jnp.float32),
        pltpu.VMEM((levels * tokens, LANES), jnp.int32),
        pltpu.VMEM((8, LANES), jnp.int32),
        pltpu.VMEM((slots // TILE, 4 * rows, TILE), jnp.float32),
        pltpu.VMEM((4 * rows, LANES), jnp.float32),
        pltpu.VMEM((4 * rows, LANES), jnp.float32),
        pltpu.VMEM((near + 1, 4 * rows, width), jnp.bfloat16),
        pltpu.VMEM((near + 1, 4 * rows, 2 * width), jnp.float32),
        pltpu.VMEM((near + 1, 4 * rows, LANES), jnp.float32),
        pltpu.VMEM((4, near + 1, packed, width), jnp.bfloat16),
        pltpu.VMEM((4, near + 1, packed, width), jnp.bfloat16),
        dma((7,)),
        dma((groups,)),
        dma((groups,)),
        dma((4, near + 1)),
        dma((4, near + 1)),
        dma((4, near + 1)),
        dma((4, near + 1)),
    ]
    return pl.pallas_call(
        functools.partial(kernel, levels, groups),
        out_shape=jax.ShapeDtypeStruct(queries.shape, queries.dtype),
        in_specs=[anywhere] * 7,
        out_specs=vmem,
        scratch_shapes=scratch,
        compiler_params=pltpu.CompilerParams(
            collective_id=0, has_side_effects=True, vmem_limit_bytes=60 * 1024 * 1024
        ),
        cost_estimate=pl.CostEstimate(
            flops=4 * levels * rows * slots * width,
            bytes_accessed=4 * slots * width,
            transcendentals=levels * rows * slots,
        ),
        name="ring_attention",
    )(queries, cache_keys, cache_values, cache_counts, new_keys, new_values, new_positions)


def solution(mesh):
    placed = (
        P("kv", "qh", "ctx", None),
        P("kv", "ctx", None),
        P("kv", "ctx", None),
        P("ctx"),
        P("kv", ("ctx", "qh"), None),
        P("kv", ("ctx", "qh"), None),
        P(),
    )
    return jax.shard_map(
        per_device,
        mesh=mesh,
        in_specs=placed,
        out_specs=P("kv", "qh", "ctx", None),
        check_vma=False,
    )
```

```python
import functools

import jax
import jax.numpy as jnp
from jax import lax
from jax.experimental import pallas as pl
from jax.experimental.pallas import tpu as pltpu
from jax.sharding import PartitionSpec as P

LOG2E = 1.4426950408889634
TILE = 2048
LANES = 128
STATS = 16


def contract(a, b, dims):
    return lax.dot_general(a, b, (dims, ((), ())), preferred_element_type=jnp.float32)


def kernel(
    levels, groups, q_hbm, k_hbm, v_hbm, count_hbm, nk_hbm, nv_hbm, pos_hbm, out_ref,
    q_ref, nk_ref, nv_ref, count_ref, pos_ref, loaded, keys, values, fresh, fresh_keys, fresh_values, wide, place_col, place_row,
    scores, extra, tops, queries, total, peaks,
    sent, landed,
    load_sem, fresh_send, fresh_recv, ag_send, ag_recv, back_send, back_recv,
):
    _, heads, tokens, width = q_ref.shape
    rows = heads * tokens
    slots = keys.shape[1]
    tiles = slots // TILE
    half = levels // 2
    near = half // 2
    members = ((0, 1, 4), (0, 1, 2)) + ((0, 1, 2, 3),) * (near - 2) + ((2, 3),)
    steps = len(members)
    streams = (0, 1, 2, 3)
    first_step = (0, 0, 1, 2)
    last_step = (near - 1, near - 1, near, near)
    sign = (1, -1, 1, -1)

    def distance(stream, step):
        return step + 1 if stream < 2 else half + 1 - step

    own_new = nk_ref.shape[1]
    factor = LOG2E * width ** -0.5
    me = lax.axis_index("ctx")
    group = lax.axis_index("qh")

    def level(offset):
        return lax.rem(me + offset + levels, levels)

    def send(src, dst, send_sem, recv_sem, where):
        return pltpu.make_async_remote_copy(
            src_ref=src, dst_ref=dst, send_sem=send_sem, recv_sem=recv_sem,
            device_id=where, device_id_type=pl.DeviceIdType.MESH,
        )

    loads = [
        pltpu.make_async_copy(src, dst, load_sem.at[i])
        for i, (src, dst) in enumerate((
            (q_hbm, q_ref), (nk_hbm, nk_ref), (nv_hbm, nv_ref), (count_hbm, count_ref), (pos_hbm, pos_ref),
            (k_hbm.at[0], loaded), (v_hbm.at[0], values.at[:, 0:width]),
        ))
    ]
    for load in loads:
        load.start()

    barrier = pltpu.get_barrier_semaphore()
    partners = (1, -1, near + 1, -near - 1, near, -near, half - 1, 1 - half, half)
    for hop in partners:
        pl.semaphore_signal(barrier, inc=1, device_id={"ctx": level(hop)}, device_id_type=pl.DeviceIdType.MESH)
    for k in range(1, groups):
        pl.semaphore_signal(
            barrier, inc=1, device_id={"qh": lax.rem(group + k, groups)}, device_id_type=pl.DeviceIdType.MESH
        )

    loads[0].wait()
    queries[0, 2 * rows:3 * rows, :] = (
        q_ref[0].astype(jnp.float32).reshape(rows, width).astype(jnp.bfloat16)
    )
    pl.semaphore_wait(barrier, len(partners) + groups - 1)

    own = queries.at[0, 2 * rows:3 * rows]

    def part(stream, step):
        at = members[step].index(stream)
        return slice(at * rows, (at + 1) * rows)

    def onward(stream):
        return sign[stream] if stream < 2 else -sign[stream]

    def query_copy(stream, step, src):
        enters = step == first_step[stream]
        hop = sign[stream] * distance(stream, step) if enters else onward(stream)
        return send(
            src, queries.at[step, part(stream, step)], ag_send.at[stream, step], ag_recv.at[stream, step],
            {"ctx": level(hop)},
        )

    for stream in streams:
        query_copy(stream, first_step[stream], own).start()

    for load in loads[1:5]:
        load.wait()
    wide[...] = jnp.zeros_like(wide)
    wide[0:own_new, :] = nk_ref[0].astype(jnp.float32)
    wide[STATS:STATS + own_new, :] = nv_ref[0].astype(jnp.float32)
    fresh[group] = wide[...].astype(jnp.bfloat16)

    def fresh_copy(k):
        return send(
            fresh.at[group], fresh.at[group], fresh_send.at[k], fresh_recv.at[group],
            {"qh": lax.rem(group + k, groups)},
        )

    def fresh_arrival(k):
        other = lax.rem(group + k, groups)
        return send(fresh.at[other], fresh.at[other], fresh_send.at[k], fresh_recv.at[other], {"qh": other})

    for k in range(1, groups):
        fresh_copy(k).start()

    def note_places(j, _):
        for i in range(tokens):
            place_col[pl.ds(j * tokens + i, 1), :] = jnp.full((1, LANES), pos_ref[j * tokens + i], jnp.int32)
        return 0

    lax.fori_loop(0, levels, note_places, 0)
    lane = lax.broadcasted_iota(jnp.int32, (8, LANES), 1)
    row = jnp.full((8, LANES), 1 << 30, jnp.int32)
    for g in range(groups):
        for i in range(own_new):
            place = pos_ref[me * tokens + g * own_new + i]
            row = jnp.where(lane == g * STATS + i, place, row)
    place_row[...] = row

    def forward(step):
        for stream in members[step]:
            if stream in streams:
                query_copy(stream, step, own).wait_recv()
                if step < last_step[stream]:
                    query_copy(stream, step + 1, queries.at[step, part(stream, step)]).start()

    count = count_ref[0]
    loads[5].wait()
    loads[6].wait()
    first_key = loaded[0:16, :].astype(jnp.float32)[0:1, :]
    chunk = 1024 if slots % 2048 == 0 else 512

    def prepare(j, _):
        base = pl.multiple_of(j * chunk, chunk)
        at = pl.ds(base, chunk)
        valid = lax.broadcasted_iota(jnp.int32, (chunk, width), 0) + base < count
        mass = jnp.where(valid, 1.0, 0.0).astype(jnp.bfloat16)
        values[at, width:2 * width] = mass
        values[at, 0:width] = values[at, 0:width] * mass
        chosen = jnp.where(valid, loaded[at, :].astype(jnp.float32), first_key)
        keys[:, at] = chosen.astype(jnp.bfloat16).T
        return 0

    lax.fori_loop(0, slots // chunk // 2, prepare, 0)
    forward(0)
    lax.fori_loop(slots // chunk // 2, slots // chunk, prepare, 0)

    fresh_keys[...] = jnp.zeros_like(fresh_keys)
    fresh_values[:, 0:width] = jnp.zeros((LANES, width), jnp.bfloat16)
    fresh_values[:, width:2 * width] = jnp.ones((LANES, width), jnp.bfloat16)
    for k in range(1, groups):
        fresh_arrival(k).wait_recv()
    for g in range(groups):
        fresh_keys[g * STATS:(g + 1) * STATS, :] = fresh[g, 0:STATS, :]
        fresh_values[g * STATS:(g + 1) * STATS, 0:width] = fresh[g, STATS:2 * STATS, :]

    def height(step):
        return len(members[step]) * rows

    def score_tile(step, j):
        at = pl.ds(pl.multiple_of(j * TILE, TILE), TILE)
        here = slice(0, height(step))
        made = contract(queries[step, here], keys[:, at], ((1,), (0,)))
        scores[j, here] = made
        top = tops[here]
        for g in range(TILE // LANES):
            top = jnp.maximum(top, made[:, g * LANES:(g + 1) * LANES])
        tops[here] = top

    def score_start():
        tops[...] = jnp.full(tops.shape, -1e30, jnp.float32)

    def score_end(step):
        here = slice(0, height(step))
        made = contract(queries[step, here], fresh_keys[...], ((1,), (1,)))

        def causal(stream):
            owner = me if stream == 4 else level(-sign[stream] * distance(stream, step))
            scored = made[part(stream, step)]
            place = place_col[pl.ds(pl.multiple_of(owner * tokens, 8), tokens), :]
            place = jnp.concatenate([place] * heads, axis=0)
            limit = jnp.broadcast_to(place_row[0:1, :], place.shape)
            return jnp.where(limit <= place, scored, -1e30)

        masked = jnp.concatenate([causal(stream) for stream in members[step]], axis=0)
        extra[here] = masked
        top = jnp.max(jnp.maximum(tops[here], masked), axis=1, keepdims=True)
        top = top.astype(jnp.bfloat16).astype(jnp.float32)
        peaks[step, here] = jnp.broadcast_to(top, (height(step), LANES))

    def weigh(made, peak):
        return [
            jnp.exp2(made[:, g * LANES:(g + 1) * LANES] * factor - peak)
            for g in range(made.shape[1] // LANES)
        ]

    def weigh_start(step):
        here = slice(0, height(step))
        weight = weigh(extra[here], peaks[step, here] * factor)[0].astype(jnp.bfloat16)
        total[step, here] = contract(weight, fresh_values[...], ((1,), (0,)))

    def weigh_tile(step, j):
        at = pl.ds(pl.multiple_of(j * TILE, TILE), TILE)
        here = slice(0, height(step))
        weight = jnp.concatenate(weigh(scores[j, here], peaks[step, here] * factor), axis=1).astype(jnp.bfloat16)
        total[step, here] += contract(weight, values[at, :], ((1,), (0,)))

    eye = lax.broadcasted_iota(jnp.int32, (rows, LANES), 0) == lax.broadcasted_iota(jnp.int32, (rows, LANES), 1)

    def pack(ref, summed):
        number, mass, peak = summed
        ref[0:rows, :] = number.astype(jnp.bfloat16)
        peak_row = jnp.sum(jnp.where(eye, peak, 0.0), axis=0, keepdims=True)
        mass_row = jnp.sum(jnp.where(eye, mass, 0.0), axis=0, keepdims=True)
        mass_high = mass_row.astype(jnp.bfloat16).astype(jnp.float32)
        line = lax.broadcasted_iota(jnp.int32, (STATS, LANES), 0)
        stats = jnp.where(
            line == 0, peak_row, jnp.where(line == 1, mass_high, jnp.where(line == 2, mass_row - mass_high, 0.0))
        )
        ref[rows:rows + STATS, :] = stats.astype(jnp.bfloat16)

    def unpack(ref):
        number = ref[0:rows, :].astype(jnp.float32)
        stats = ref[rows:rows + STATS, :].astype(jnp.float32)

        def column(line):
            spread = jnp.where(eye, jnp.broadcast_to(line, (rows, LANES)), 0.0)
            return jnp.broadcast_to(jnp.sum(spread, axis=1, keepdims=True), (rows, LANES))

        return number, column(stats[1:2, :] + stats[2:3, :]), column(stats[0:1, :])

    def local(step, stream):
        at = part(stream, step)
        return total[step, at, 0:width], total[step, at, width:2 * width], peaks[step, at, :]

    def merge(a, b):
        peak = jnp.maximum(a[2], b[2])
        wa = jnp.exp2((a[2] - peak) * factor)
        wb = jnp.exp2((b[2] - peak) * factor)
        return a[0] * wa + b[0] * wb, a[1] * wa + b[1] * wb, peak

    def back_copy(stream, step):
        hop = -sign[stream] * distance(stream, step) if step == last_step[stream] else onward(stream)
        return send(
            sent.at[stream, step], landed.at[stream, step], back_send.at[stream, step], back_recv.at[stream, step],
            {"ctx": level(hop)},
        )

    def pass_on(stream, step):
        summed = local(step, stream)
        if step > first_step[stream]:
            back_copy(stream, step - 1).wait_recv()
            summed = merge(summed, unpack(landed.at[stream, step - 1]))
        pack(sent.at[stream, step], summed)
        back_copy(stream, step).start()

    def every(count, body):
        lax.fori_loop(0, count, lambda i, _: (body(i), 0)[1], 0)

    score_start()
    every(tiles, lambda j: score_tile(0, j))
    score_end(0)
    forward(1)
    for step in range(steps):
        weigh_start(step)
        if step < steps - 1:
            score_start()

            def both(j):
                weigh_tile(step, j)
                score_tile(step + 1, j)

            every(tiles, both)
            score_end(step + 1)
            if step < steps - 2:
                forward(step + 2)
        else:
            every(tiles, lambda j: weigh_tile(step, j))
        for stream in reversed(members[step]):
            if stream in streams:
                pass_on(stream, step)

    result = local(0, 4)
    for stream in streams:
        back_copy(stream, last_step[stream]).wait_recv()
        result = merge(result, unpack(landed.at[stream, last_step[stream]]))
    out_ref[0] = (result[0] / result[1]).reshape(heads, tokens, width).astype(jnp.bfloat16)

    for stream in streams:
        for step in range(first_step[stream], last_step[stream] + 1):
            query_copy(stream, step, own).wait_send()
            back_copy(stream, step).wait_send()
    for k in range(1, groups):
        fresh_copy(k).wait_send()


def per_device(queries, cache_keys, cache_values, cache_counts, new_keys, new_values, new_positions):
    levels = lax.axis_size("ctx")
    groups = lax.axis_size("qh")
    _, heads, tokens, width = queries.shape
    slots = cache_keys.shape[1]
    rows = heads * tokens
    near = levels // 4
    vmem = pl.BlockSpec(memory_space=pltpu.VMEM)
    anywhere = pl.BlockSpec(memory_space=pl.ANY)
    packed = rows + STATS
    dma = pltpu.SemaphoreType.DMA
    scratch = [
        pltpu.VMEM(queries.shape, queries.dtype),
        pltpu.VMEM(new_keys.shape, new_keys.dtype),
        pltpu.VMEM(new_values.shape, new_values.dtype),
        pltpu.SMEM(cache_counts.shape, cache_counts.dtype),
        pltpu.SMEM(new_positions.shape, new_positions.dtype),
        pltpu.VMEM((slots, width), jnp.bfloat16),
        pltpu.VMEM((width, slots), jnp.bfloat16),
        pltpu.VMEM((slots, 2 * width), jnp.bfloat16),
        pltpu.VMEM((groups, 2 * STATS, width), jnp.bfloat16),
        pltpu.VMEM((LANES, width), jnp.bfloat16),
        pltpu.VMEM((LANES, 2 * width), jnp.bfloat16),
        pltpu.VMEM((2 * STATS, width), jnp.float32),
        pltpu.VMEM((levels * tokens, LANES), jnp.int32),
        pltpu.VMEM((8, LANES), jnp.int32),
        pltpu.VMEM((slots // TILE, 4 * rows, TILE), jnp.float32),
        pltpu.VMEM((4 * rows, LANES), jnp.float32),
        pltpu.VMEM((4 * rows, LANES), jnp.float32),
        pltpu.VMEM((near + 1, 4 * rows, width), jnp.bfloat16),
        pltpu.VMEM((near + 1, 4 * rows, 2 * width), jnp.float32),
        pltpu.VMEM((near + 1, 4 * rows, LANES), jnp.float32),
        pltpu.VMEM((4, near + 1, packed, width), jnp.bfloat16),
        pltpu.VMEM((4, near + 1, packed, width), jnp.bfloat16),
        dma((7,)),
        dma((groups,)),
        dma((groups,)),
        dma((4, near + 1)),
        dma((4, near + 1)),
        dma((4, near + 1)),
        dma((4, near + 1)),
    ]
    return pl.pallas_call(
        functools.partial(kernel, levels, groups),
        out_shape=jax.ShapeDtypeStruct(queries.shape, queries.dtype),
        in_specs=[anywhere] * 7,
        out_specs=vmem,
        scratch_shapes=scratch,
        compiler_params=pltpu.CompilerParams(
            collective_id=0, has_side_effects=True, vmem_limit_bytes=60 * 1024 * 1024
        ),
        cost_estimate=pl.CostEstimate(
            flops=4 * levels * rows * slots * width,
            bytes_accessed=4 * slots * width,
            transcendentals=levels * rows * slots,
        ),
        name="ring_attention",
    )(queries, cache_keys, cache_values, cache_counts, new_keys, new_values, new_positions)


def solution(mesh):
    placed = (
        P("kv", "qh", "ctx", None),
        P("kv", "ctx", None),
        P("kv", "ctx", None),
        P("ctx"),
        P("kv", ("ctx", "qh"), None),
        P("kv", ("ctx", "qh"), None),
        P(),
    )
    return jax.shard_map(
        per_device,
        mesh=mesh,
        in_specs=placed,
        out_specs=P("kv", "qh", "ctx", None),
        check_vma=False,
    )
```
